128 devices in a mesh: space: 32 (over y, x_hi, z), species: 4 (over x_lo, core).
Axes of the slice: x: 4 (x_hi: 2, x_lo: 2; x = x_hi * 2 + x_lo), y: 4, z: 4, core: 2. Of those that a mesh axis runs over, the one named last changes fastest.
Arguments:
- effects: float32 [192, 256, 2048], P('space', None, 'species'), may hold values from -1.2 to 1.2
- kappa_sq: float32 [192, 256], P('space'), may hold values from 0.1 to 2
- growth: float32 [192, 256, 128], P('space'), may hold values from -6 to 6
- tree_species: int32 [192, 256, 128], P('space'), may hold values from 0 to 2047
- tree_counts: int32 [192, 256], P('space'), may hold values from 1 to 128, as said below
- noise_precision: float32 [2048], P('species'), may hold values from 0.5 to 4
- species_precision: bfloat16 [2048, 2048], P(None, 'species'), as said below
Outputs:
- grad_effects: float32 [192, 256, 2048], P('space', None, 'species')
- gram: float32 [2048, 2048], P('space', 'species')
The draws below stay inside these ranges and needn't reach their ends.
Inputs may be any that keep to these rules, and one draw needn't show every extreme that they name: `tree_counts`: some plot has 128 live trees. species_precision is symmetric.
All inputs are finite; a program needn't handle non-finite values.
Results may differ from the reference program's by a relative error of at most 0.0029.
Values may be sent and summed in bfloat16 or wider, within the bound.
A program may use at most 128 MiB of HBM per device.

```python
import math
import jax
import jax.numpy as jnp
import numpy as np
from jax import lax

S = 2048
GC = 256
TREES = 128
GRID_R = 192
NPLOTS = 49152


def draw_tree_counts(key, part):
    drawn_counts = jax.random.randint(key, (GRID_R, GC), 1, TREES + 1)
    flat_index = lax.broadcasted_iota(jnp.int32, (GRID_R, GC), 0) * GC + lax.broadcasted_iota(jnp.int32, (GRID_R, GC), 1)
    return jnp.where(flat_index % 64 == 0, TREES, drawn_counts).astype(jnp.int32)


def draw_species_precision(key, part):
    first_key, second_key = jax.random.split(jax.random.fold_in(key, 7))
    base_draw = jax.random.normal(first_key, (S, S), jnp.float32)
    diagonal_draw = jax.random.uniform(second_key, (S,), jnp.float32, 1.0, 2.0)
    identity = (lax.broadcasted_iota(jnp.int32, (S, S), 0) == lax.broadcasted_iota(jnp.int32, (S, S), 1)).astype(jnp.float32)
    off_part = (base_draw + base_draw.T) * (0.25 / math.sqrt(S))
    result_matrix = off_part * (1.0 - identity) + identity * diagonal_draw[:, None]
    return result_matrix.astype(jnp.bfloat16)


def set_ends(drawn, stream_key, smallest, largest):
    longest = drawn.shape.index(max(drawn.shape))
    spots = []
    for shift in (0, 1):
        where = [jax.random.randint(jax.random.fold_in(stream_key, axis), (), 0, length) for axis, length in enumerate(drawn.shape)]
        where[longest] = (where[longest] + shift) % drawn.shape[longest]
        spots.append(tuple(where))
    return drawn.at[spots[0]].set(smallest).at[spots[1]].set(largest)


def block_levels(stream_key, shape, shards, smallest, high):
    def one(axis_at, blocks):
        draws = jax.random.uniform(jax.random.fold_in(jax.random.fold_in(stream_key, 6), axis_at), (blocks,), jnp.float32, smallest / len(shards), high / len(shards))
        return jnp.repeat(jnp.exp(draws), shape[axis_at] // blocks).reshape((-1,) + (1,) * (len(shape) - axis_at - 1))

    level = one(*shards[0])
    for cut in shards[1:]:
        level = level * one(*cut)
    return level


def rank_bounds(number_of, slope):
    loads = [(1 << 20) // math.isqrt(grade ** slope) + 1 for grade in range(1, number_of + 1)]
    width = 1 + sum(loads) // (1 << 30)
    return np.cumsum(np.array([max(1, weight // width) for weight in loads]))


def skewed_ids(rng, shape, number_of, slope):
    table = rank_bounds(number_of, slope)
    ticket = jax.random.randint(jax.random.fold_in(rng, 1), shape, 0, int(table[number_of - 1]))
    standing = jnp.searchsorted(jnp.asarray(table, jnp.int32), ticket, side="right")
    return jax.random.permutation(jax.random.fold_in(rng, 2), number_of)[standing].astype(jnp.int32)


def centred(own_key, extent, deviation, most, cuts=(), kind=jnp.bfloat16):
    array = deviation * jax.random.normal(own_key, extent, jnp.float32)
    if cuts:
        array = array * block_levels(own_key, extent, cuts, -0.22, 0.18)
    return jnp.clip(array, -most, most).astype(kind)


def setup_inputs(seed: int = 0) -> dict:
    key_of = jax.random.split(jax.random.key(seed), 8)
    effects = centred(key_of[0], (GRID_R, GC, S), 0.2, 1.2, ((0, 32), (2, 4)), jnp.float32)
    kappa_sq = jnp.clip(jnp.exp(math.log(2.0) - 2.9957323 * jax.random.uniform(key_of[1], (GRID_R, GC), jnp.float32) ** block_levels(key_of[1], (GRID_R, GC), ((0, 32),), -0.2, 0.2)), 0.1, 2.0)
    growth = centred(key_of[2], (GRID_R, GC, TREES), 1.0, 6.0, ((0, 32),), jnp.float32)
    tree_species = set_ends(skewed_ids(key_of[3], (GRID_R, GC, TREES), S, 2), jax.random.fold_in(key_of[3], 3), 0, S - 1).astype(jnp.int32)
    tree_counts = draw_tree_counts(jax.random.fold_in(key_of[7], 71), 0)
    noise_precision = jnp.clip(jnp.exp(math.log(4.0) - 2.0794415 * jax.random.uniform(key_of[5], (S,), jnp.float32) ** block_levels(key_of[5], (S,), ((0, 4),), -0.2, 0.2)), 0.5, 4.0)
    species_precision = draw_species_precision(jax.random.fold_in(key_of[7], 71), 0)
    return dict(effects=effects, kappa_sq=kappa_sq, growth=growth, tree_species=tree_species, tree_counts=tree_counts, noise_precision=noise_precision, species_precision=species_precision)


def apply_k(field_in, kappa_grid):
    padded = jnp.pad(field_in, ((1, 1), (1, 1), (0, 0)))
    beside = padded[2:, 1:-1] + padded[:-2, 1:-1] + padded[1:-1, 2:] + padded[1:-1, :-2]
    return (kappa_grid[..., None] + 4.0) * field_in - beside


def reference(effects, kappa_sq, growth, tree_species, tree_counts, noise_precision, species_precision):
    spatial = apply_k(apply_k(effects, kappa_sq), kappa_sq)
    spatial_low = spatial.astype(jnp.bfloat16).astype(jnp.float32).reshape(NPLOTS, S)
    effects_low = effects.astype(jnp.bfloat16).astype(jnp.float32).reshape(NPLOTS, S)
    precision_wide = species_precision.astype(jnp.float32)
    prior_term = jnp.dot(spatial_low, precision_wide, precision=lax.Precision.HIGHEST)
    growth_low = growth.astype(jnp.bfloat16).astype(jnp.float32)
    live_tree = lax.broadcasted_iota(jnp.int32, (GRID_R, GC, TREES), 2) < tree_counts[..., None]
    plot_index = lax.broadcasted_iota(jnp.int32, (NPLOTS, TREES), 0)
    species_flat = tree_species.reshape(NPLOTS, TREES)
    live_flat = live_tree.reshape(NPLOTS, TREES)
    growth_sum = jnp.zeros((NPLOTS, S), jnp.float32).at[plot_index, species_flat].add(jnp.where(live_flat, growth_low.reshape(NPLOTS, TREES), jnp.float32(0.0)))
    tally = jnp.zeros((NPLOTS, S), jnp.float32).at[plot_index, species_flat].add(jnp.where(live_flat, jnp.float32(1.0), jnp.float32(0.0)))
    grad_flat = noise_precision[None, :] * (growth_sum - tally * effects.reshape(NPLOTS, S)) - prior_term
    gram = jnp.dot(effects_low.T, spatial_low, precision=lax.Precision.HIGHEST) * (-0.5 / NPLOTS)
    return grad_flat.reshape(GRID_R, GC, S), gram
```

```python
import jax
import jax.numpy as jnp
from jax import lax
from jax.experimental import pallas as pl
from jax.experimental.pallas import tpu as pltpu
from jax.sharding import PartitionSpec as P

MESH = pl.DeviceIdType.MESH
BF = jnp.bfloat16
F32 = jnp.float32
R, C, W, T = 6, 256, 512, 128
NP = R * C
GROUP = 32
CHUNKS = ((2, 2), (1, 1), (4, 1), (0, 1), (5, 1))


def kernel(
    eff, kap, growth, species, counts, noise, prec,
    out, gram,
    halo, kap_up, kap_dn, tmp, kap_b, cnt_b, first, spat, eff_t, sums,
    part, rz, ry, mid0, mid1, rz2, ry2, held, rx, fin,
    halo_s, halo_r, ex_s, ex_r, gz_s, gz_r, gy_s, gy_r, g2y_s, g2y_r, g2z_s, g2z_r, last_s, last_r, loc,
):
    sp, me = lax.axis_index("space"), lax.axis_index("species")
    z, xh, y = sp % 4, (sp // 4) % 2, sp // 8
    up, dn = (sp + 31) % 32, (sp + 1) % 32
    sib = (me // 2) * 2 + (me + 1) % 2
    far = (me + 2) % 4

    def at(yy, hh, zz):
        return (yy * 2 + hh) * 4 + zz

    def dev(space, spec):
        return {"space": space, "species": spec}

    def block(k):
        return ((me // 2 + k // 2) % 2) * 2 + (me % 2 + k % 2) % 2

    mine = ((me // 2 + y // 2) % 2) * 2 + (me % 2 + y % 2) % 2
    moved = y != me

    def remote(src, dst, ssem, rsem, to):
        return pltpu.make_async_remote_copy(
            src_ref=src, dst_ref=dst, send_sem=ssem, recv_sem=rsem, device_id=to, device_id_type=MESH
        )

    barrier = pltpu.get_barrier_semaphore()
    peers = [dev(up, me), dev(dn, me), dev(sp, sib), dev(sp, far), dev(at(y, 1 - xh, z), me)]
    peers += [dev(at(y, xh, (z + d) % 4), me) for d in (1, 2, 3)]
    peers += [dev(at((y + d) % 4, xh, z), me) for d in (1, 2, 3)]
    for peer in peers:
        pl.semaphore_signal(barrier, inc=1, device_id=peer, device_id_type=MESH)
    swap = dev(at(me, xh, z), y)

    @pl.when(moved)
    def _():
        pl.semaphore_signal(barrier, inc=1, device_id=swap, device_id_type=MESH)

    tmp[...] = jnp.zeros_like(tmp)
    tmp[0:R, :] = kap[...]
    kap_cols = tmp[...].T
    for r in range(R):
        kap_b[r + 1] = jnp.broadcast_to(kap_cols[:, r : r + 1], (C, T)) + 4.0
    tmp[0:R, :] = counts[...].astype(F32)
    cnt_cols = tmp[...].T
    for r in range(R):
        cnt_b[r * C : (r + 1) * C, :] = jnp.broadcast_to(cnt_cols[:, r : r + 1], (C, T)).astype(jnp.int32)

    pl.semaphore_wait(barrier, len(peers) + moved.astype(jnp.int32))

    def row(r):
        return eff.at[pl.ds(r * C, C)]

    halos = [
        remote(row(0), halo.at[2], halo_s.at[0], halo_r.at[0], dev(up, me)),
        remote(row(5), halo.at[1], halo_s.at[1], halo_r.at[1], dev(dn, me)),
        remote(kap, kap_dn, halo_s.at[2], halo_r.at[2], dev(up, me)),
        remote(kap, kap_up, halo_s.at[3], halo_r.at[3], dev(dn, me)),
        remote(row(1), halo.at[3], halo_s.at[4], halo_r.at[4], dev(up, me)),
        remote(row(4), halo.at[0], halo_s.at[5], halo_r.at[5], dev(dn, me)),
    ]
    for copy in halos:
        copy.start()

    def erow(r):
        if 0 <= r < R:
            return row(r)
        return halo.at[r + 2 if r < 0 else r - 4]

    edge = lax.broadcasted_iota(jnp.int32, (C, T), 0)

    def stencil(centre, above, below, kappa):
        left = jnp.where(edge == 0, 0.0, pltpu.roll(centre, 1, 0))
        right = jnp.where(edge == C - 1, 0.0, pltpu.roll(centre, C - 1, 0))
        return kappa * centre - (below + above + right + left)

    def first_row(r):
        def body(c, carry):
            cs = pl.ds(pl.multiple_of(c * T, T), T)
            first[r + 1, :, cs] = stencil(erow(r)[:, cs], erow(r - 1)[:, cs], erow(r + 1)[:, cs], kap_b[r + 1])
            return carry

        lax.fori_loop(0, W // T, body, 0)

    def spat_row(r):
        def body(c, carry):
            cs = pl.ds(pl.multiple_of(c * T, T), T)
            s = stencil(first[r + 1, :, cs], first[r, :, cs], first[r + 2, :, cs], kap_b[r + 1])
            spat[0, r * C : (r + 1) * C, cs] = s.astype(BF)
            return carry

        lax.fori_loop(0, W // T, body, 0)

    def piece(k, i):
        r, n = CHUNKS[i]
        return spat.at[k, pl.ds(r * C, n * C)]

    def to_sib(i):
        return remote(piece(0, i), piece(1, i), ex_s.at[0, i], ex_r.at[0, i], dev(sp, sib))

    def to_far(i):
        return remote(piece(0, i), piece(2, i), ex_s.at[1, i], ex_r.at[1, i], dev(sp, far))

    def on(i):
        return remote(piece(2, i), piece(3, i), ex_s.at[2, i], ex_r.at[2, i], dev(sp, sib))

    def send(*chunks):
        for i in chunks:
            to_far(i).start()
            to_sib(i).start()

    lane = lax.broadcasted_iota(jnp.int32, (8, T), 1)
    low_iota = lax.broadcasted_iota(jnp.int32, (T, T), 0)
    sub = lax.broadcasted_iota(jnp.int32, (8, T), 0)
    nothing = jnp.zeros((8, T), F32)

    def trees(row_lo, row_hi):
        def step(g, r):
            start = r * C + g * GROUP
            for q in range(GROUP // 8):
                rows = pl.ds(pl.multiple_of(start + q * 8, 8), 8)
                ids = species[rows, :]
                live = lane < cnt_b[rows, :]
                high = jnp.where(live, lax.shift_right_arithmetic(ids, 7) - 4 * me, -1)
                low = ids & 127
                value = growth[rows, :].astype(BF).astype(F32)

                def left_side(p):
                    chosen = jnp.broadcast_to(high[p : p + 1, :], (8, T)) == (sub & 3)
                    held_value = jnp.where(sub < 4, jnp.broadcast_to(value[p : p + 1, :], (8, T)), 1.0)
                    return jnp.where(chosen, held_value, 0.0)

                def right_side(p):
                    same = jnp.broadcast_to(low[p : p + 1, :], (T, T)) == low_iota
                    return jnp.where(same, 1.0, 0.0).astype(BF)

                for p in range(0, 8, 2):
                    a = jnp.concatenate(
                        [
                            jnp.concatenate([left_side(p), nothing], 1),
                            jnp.concatenate([nothing, left_side(p + 1)], 1),
                        ],
                        0,
                    ).astype(BF)
                    b = jnp.concatenate([right_side(p), right_side(p + 1)], 1)
                    both = lax.dot_general(a, b, (((1,), (1,)), ((), ())), preferred_element_type=F32)
                    for j in range(2):
                        sums[pl.ds(g * GROUP + q * 8 + p + j, 8, stride=C), :] = both[j * 8 : (j + 1) * 8, :]
            return r

        def whole(r, carry):
            lax.fori_loop(0, C // GROUP, step, r)
            rows = pl.ds(pl.multiple_of(r * C, C), C)
            for h in range(4):
                cs = slice(h * T, (h + 1) * T)
                total = sums[h * C : (h + 1) * C, :]
                tally = sums[(h + 4) * C : (h + 5) * C, :]
                out[rows, cs] = noise[:, cs] * (total - tally * eff[rows, cs])
            return carry

        lax.fori_loop(row_lo, row_hi, whole, 0)

    def prior(ks):
        def body(i, carry):
            rows = pl.ds(pl.multiple_of(i * 512, 512), 512)
            total = None
            for k in ks:
                q = prec[pl.ds(pl.multiple_of(block(k) * W, W), W), :]
                term = jnp.dot(spat[k, rows, :], q, preferred_element_type=F32)
                total = term if total is None else total + term
            out[rows, :] = out[rows, :] - total
            return carry

        lax.fori_loop(0, NP // 512, body, 0)

    def gram_block(k):
        def body(i, carry):
            cs = pl.ds(pl.multiple_of(i * 256, 256), 256)
            part[k, :, cs] = jnp.dot(eff_t[...], spat[k, :, cs], preferred_element_type=F32).astype(BF)
            return carry

        lax.fori_loop(0, W // 256, body, 0)

    def z_peer(d):
        return dev(at(y, xh, (z + d) % 4), me)

    def gz(k, d):
        src = part.at[k, pl.ds(pl.multiple_of(((z + d) % 4) * 64, 64), 64)]
        return remote(src, rz.at[d - 1, k], gz_s.at[k, d - 1], gz_r.at[k, d - 1], z_peer(d))

    def gy(k):
        d = (block(k) - y + 4) % 4
        slot = (d + 3) % 4
        return remote(part.at[k, pl.ds(256, 256)], ry.at[slot], gy_s.at[k], gy_r.at[slot], dev(at(block(k), xh, z), me))

    def gram_send(k):
        for d in (1, 2, 3):
            gz(k, d).start()

        @pl.when(block(k) != y)
        def _():
            gy(k).start()

    def g2y(k):
        d = (block(k) - y + 4) % 4
        slot = (d + 3) % 4
        return remote(mid0.at[k], ry2.at[slot], g2y_s.at[k], g2y_r.at[slot], dev(at(block(k), xh, z), me))

    def g2z(d):
        src = mid1.at[pl.ds(pl.multiple_of(((z + d) % 4) * 64, 64), 64)]
        return remote(src, rz2.at[d - 1], g2z_s.at[d - 1], g2z_r.at[d - 1], z_peer(d))

    for r in (1, 2, 3, 4):
        first_row(r)
    spat_row(2)
    spat_row(3)
    send(0)
    trees(0, 2)

    for i in range(4):
        halos[i].wait_recv()
    tmp[0:1, :] = kap_up[R - 1 : R, :]
    tmp[1:2, :] = kap_dn[0:1, :]
    kap_edge = tmp[...].T
    kap_b[0] = jnp.broadcast_to(kap_edge[:, 0:1], (C, T)) + 4.0
    kap_b[R + 1] = jnp.broadcast_to(kap_edge[:, 1:2], (C, T)) + 4.0

    @pl.when(sp == 0)
    def _():
        halo[1] = jnp.zeros((C, W), F32)

    @pl.when(sp == 31)
    def _():
        halo[2] = jnp.zeros((C, W), F32)

    first_row(0)
    first_row(5)
    spat_row(1)
    spat_row(4)
    send(1, 2)
    trees(2, 4)

    halos[4].wait_recv()
    halos[5].wait_recv()
    first_row(-1)
    first_row(6)

    @pl.when(sp == 0)
    def _():
        first[0] = jnp.zeros((C, W), F32)

    @pl.when(sp == 31)
    def _():
        first[R + 1] = jnp.zeros((C, W), F32)

    spat_row(0)
    spat_row(5)
    send(3, 4)

    to_far(0).wait_recv()
    on(0).start()

    for r in range(R):
        eff_t[:, r * C : (r + 1) * C] = eff[r * C : (r + 1) * C, :].T.astype(BF)
    gram_block(0)
    gram_send(0)
    for i in range(5):
        to_sib(i).wait_recv()
    gram_block(1)
    gram_send(1)
    trees(4, 6)
    prior((0, 1))

    for i in range(1, 5):
        to_far(i).wait_recv()
        on(i).start()
    gram_block(2)
    gram_send(2)
    for i in range(5):
        on(i).wait_recv()
    gram_block(3)
    gram_send(3)
    prior((2, 3))

    own_rows = pl.ds(pl.multiple_of(z * 64, 64), 64)
    for k in range(4):
        for d in (1, 2, 3):
            gz(k, d).wait_recv()
        total = part[k, own_rows, :].astype(F32)
        for d in (1, 2, 3):
            total = total + rz[d - 1, k].astype(F32)
        mid0[k] = total.astype(BF)

        @pl.when(block(k) != y)
        def _():
            g2y(k).start()

    for slot in range(3):
        remote(ry.at[slot], ry.at[slot], gy_s.at[0], gy_r.at[slot], dev(sp, sib)).wait_recv()
    for q in range(4):
        rows = slice(q * 64, (q + 1) * 64)
        total = part[mine, 256 + q * 64 : 256 + (q + 1) * 64, :].astype(F32)
        for slot in range(3):
            total = total + ry[slot, rows, :].astype(F32)
        mid1[rows, :] = total.astype(BF)
    for d in (1, 2, 3):
        g2z(d).start()

    for slot in range(3):
        remote(ry2.at[slot], ry2.at[slot], g2y_s.at[0], g2y_r.at[slot], dev(sp, sib)).wait_recv()
    total = mid0[mine].astype(F32)
    for slot in range(3):
        total = total + ry2[slot].astype(F32)
    held[0] = total
    for d in (1, 2, 3):
        g2z(d).wait_recv()
    total = mid1[own_rows, :].astype(F32)
    for d in (1, 2, 3):
        total = total + rz2[d - 1].astype(F32)
    held[1] = total

    over = remote(held.at[1 - xh], rx, last_s.at[0], last_r.at[0], dev(at(y, 1 - xh, z), me))
    over.start()
    over.wait_recv()
    fin[...] = (held[xh] + rx[...]) * (-0.5 / (NP * 32))

    final = remote(fin, gram, last_s.at[1], last_r.at[1], swap)

    @pl.when(moved)
    def _():
        final.start()
        final.wait_recv()
        final.wait_send()

    @pl.when(jnp.logical_not(moved))
    def _():
        gram[...] = fin[...]

    for copy in halos:
        copy.wait_send()
    for i in range(5):
        to_sib(i).wait_send()
        to_far(i).wait_send()
        on(i).wait_send()
    for k in range(4):
        for d in (1, 2, 3):
            gz(k, d).wait_send()

        @pl.when(block(k) != y)
        def _():
            gy(k).wait_send()
            g2y(k).wait_send()

    for d in (1, 2, 3):
        g2z(d).wait_send()
    over.wait_send()


def shards(effects, kappa_sq, growth, tree_species, tree_counts, noise_precision, species_precision):
    vmem = pl.BlockSpec(memory_space=pltpu.VMEM)
    dma = pltpu.SemaphoreType.DMA
    grad, gram = pl.pallas_call(
        kernel,
        out_shape=(jax.ShapeDtypeStruct((NP, W), F32), jax.ShapeDtypeStruct((64, W), F32)),
        in_specs=[vmem] * 7,
        out_specs=(vmem, vmem),
        scratch_shapes=[
            pltpu.VMEM((4, C, W), F32),
            pltpu.VMEM((R, C), F32),
            pltpu.VMEM((R, C), F32),
            pltpu.VMEM((8, C), F32),
            pltpu.VMEM((R + 2, C, T), F32),
            pltpu.VMEM((NP, T), jnp.int32),
            pltpu.VMEM((R + 2, C, W), F32),
            pltpu.VMEM((4, NP, W), BF),
            pltpu.VMEM((W, NP), BF),
            pltpu.VMEM((8 * C, T), F32),
            pltpu.VMEM((4, W, W), BF),
            pltpu.VMEM((3, 4, 64, W), BF),
            pltpu.VMEM((3, 256, W), BF),
            pltpu.VMEM((4, 64, W), BF),
            pltpu.VMEM((256, W), BF),
            pltpu.VMEM((3, 64, W), BF),
            pltpu.VMEM((3, 64, W), BF),
            pltpu.VMEM((2, 64, W), F32),
            pltpu.VMEM((64, W), F32),
            pltpu.VMEM((64, W), F32),
            dma((6,)), dma((6,)),
            dma((3, 5)), dma((3, 5)),
            dma((4, 3)), dma((4, 3)),
            dma((4,)), dma((3,)),
            dma((4,)), dma((3,)),
            dma((3,)), dma((3,)),
            dma((2,)), dma((2,)),
            dma((1,)),
        ],
        compiler_params=pltpu.CompilerParams(
            collective_id=0, has_side_effects=True, vmem_limit_bytes=56 << 20
        ),
        cost_estimate=pl.CostEstimate(flops=7_000_000_000, bytes_accessed=12_000_000, transcendentals=0),
        name="posterior_gradient",
    )(
        effects.reshape(NP, W),
        kappa_sq,
        growth.reshape(NP, T),
        tree_species.reshape(NP, T),
        tree_counts,
        noise_precision.reshape(1, W),
        species_precision,
    )
    return grad.reshape(R, C, W), gram


def solution(mesh):
    return jax.shard_map(
        shards,
        mesh=mesh,
        in_specs=(
            P("space", None, "species"),
            P("space", None),
            P("space", None, None),
            P("space", None, None),
            P("space", None),
            P("species"),
            P(None, "species"),
        ),
        out_specs=(P("space", None, "species"), P("space", "species")),
        check_vma=False,
    )
```

```python
import jax
import jax.numpy as jnp
from jax import lax
from jax.experimental import pallas as pl
from jax.experimental.pallas import tpu as pltpu
from jax.sharding import PartitionSpec as P

MESH = pl.DeviceIdType.MESH
BF = jnp.bfloat16
F32 = jnp.float32
R, C, W, T = 6, 256, 512, 128
NP = R * C
GROUP = 32
CHUNKS = ((2, 2), (1, 1), (4, 1), (0, 1), (5, 1))


def kernel(
    eff_in, kap, growth_in, species_in, counts, noise, prec_in,
    out_hbm, gram,
    eff, growth, species, prec, out,
    near, far_out, far_in, kap_up, kap_dn, tmp, kap_b, cnt_b, first, spat, eff_t, sums,
    part, late, rz, ry, mid0, mid1, rz2, ry2, held, fin,
    halo_s, halo_r, ex_s, ex_r, gz_s, gz_r, gy_s, gy_r, g2y_s, g2y_r, g2z_s, g2z_r, last_s, last_r, in_sem, out_sem,
):
    sp, me = lax.axis_index("space"), lax.axis_index("species")
    z, xh, y = sp % 4, (sp // 4) % 2, sp // 8
    up, dn = (sp + 31) % 32, (sp + 1) % 32
    sib = (me // 2) * 2 + (me + 1) % 2
    far = (me + 2) % 4

    def at(yy, hh, zz):
        return (yy * 2 + hh) * 4 + zz

    def dev(space, spec):
        return {"space": space, "species": spec}

    def block(k):
        return ((me // 2 + k // 2) % 2) * 2 + (me % 2 + k % 2) % 2

    mine = ((me // 2 + y // 2) % 2) * 2 + (me % 2 + y % 2) % 2
    moved = y != me

    def remote(src, dst, ssem, rsem, to):
        return pltpu.make_async_remote_copy(
            src_ref=src, dst_ref=dst, send_sem=ssem, recv_sem=rsem, device_id=to, device_id_type=MESH
        )

    barrier = pltpu.get_barrier_semaphore()
    peers = [dev(up, me), dev(dn, me), dev(sp, sib), dev(sp, far), dev(at(me, 1 - xh, z), y)]
    peers += [dev(at(y, xh, (z + d) % 4), me) for d in (1, 2, 3)]
    peers += [dev(at((y + d) % 4, xh, z), me) for d in (1, 2, 3)]
    for peer in peers:
        pl.semaphore_signal(barrier, inc=1, device_id=peer, device_id_type=MESH)
    swap = dev(at(me, xh, z), y)

    @pl.when(moved)
    def _():
        pl.semaphore_signal(barrier, inc=1, device_id=swap, device_id_type=MESH)

    loads = [pltpu.make_async_copy(eff_in.at[pl.ds(r * C, C)], eff.at[pl.ds(r * C, C)], in_sem.at[r]) for r in range(R)]
    for r in (1, 4, 2, 3, 0, 5):
        loads[r].start()
    load_species = pltpu.make_async_copy(species_in, species, in_sem.at[R])
    load_growth = pltpu.make_async_copy(growth_in, growth, in_sem.at[R + 1])
    load_prec = pltpu.make_async_copy(prec_in, prec, in_sem.at[R + 2])
    load_species.start()
    load_growth.start()
    load_prec.start()

    pl.semaphore_wait(barrier, len(peers) + moved.astype(jnp.int32))

    def far_row(i):
        return remote(
            far_out.at[i], far_in.at[i], halo_s.at[4 + i], halo_r.at[4 + i], dev(up if i == 0 else dn, me)
        )

    halos = [
        remote(eff_in.at[pl.ds(0, C)], near.at[1], halo_s.at[0], halo_r.at[0], dev(up, me)),
        remote(eff_in.at[pl.ds(5 * C, C)], near.at[0], halo_s.at[1], halo_r.at[1], dev(dn, me)),
        remote(kap, kap_dn, halo_s.at[2], halo_r.at[2], dev(up, me)),
        remote(kap, kap_up, halo_s.at[3], halo_r.at[3], dev(dn, me)),
        far_row(0),
        far_row(1),
    ]
    for copy in halos[:4]:
        copy.start()
    for i, r in enumerate((1, 4)):
        loads[r].wait()
        far_out[i] = eff[r * C : (r + 1) * C, :].astype(BF)
        halos[4 + i].start()

    tmp[...] = jnp.zeros_like(tmp)
    tmp[0:R, :] = kap[...]
    kap_cols = tmp[...].T
    for r in range(R):
        kap_b[r + 1] = jnp.broadcast_to(kap_cols[:, r : r + 1], (C, T)) + 4.0

    for r in (2, 3, 0, 5):
        loads[r].wait()

    def erow(r):
        if 0 <= r < R:
            return eff.at[pl.ds(r * C, C)]
        return {-2: far_in.at[1], -1: near.at[0], 6: near.at[1], 7: far_in.at[0]}[r]

    edge = lax.broadcasted_iota(jnp.int32, (C, T), 0)

    def stencil(centre, above, below, kappa):
        left = jnp.where(edge == 0, 0.0, pltpu.roll(centre, 1, 0))
        right = jnp.where(edge == C - 1, 0.0, pltpu.roll(centre, C - 1, 0))
        return kappa * centre - (below + above + right + left)

    def first_row(r):
        def body(c, carry):
            cs = pl.ds(pl.multiple_of(c * T, T), T)
            first[r + 1, :, cs] = stencil(
                erow(r)[:, cs], erow(r - 1)[:, cs].astype(F32), erow(r + 1)[:, cs].astype(F32), kap_b[r + 1]
            )
            return carry

        lax.fori_loop(0, W // T, body, 0)

    def spat_row(r):
        def body(c, carry):
            cs = pl.ds(pl.multiple_of(c * T, T), T)
            s = stencil(first[r + 1, :, cs], first[r, :, cs], first[r + 2, :, cs], kap_b[r + 1])
            spat[0, r * C : (r + 1) * C, cs] = s.astype(BF)
            return carry

        lax.fori_loop(0, W // T, body, 0)

    def piece(k, i):
        r, n = CHUNKS[i]
        return spat.at[k, pl.ds(r * C, n * C)]

    def to_sib(i):
        return remote(piece(0, i), piece(1, i), ex_s.at[0, i], ex_r.at[0, i], dev(sp, sib))

    def to_far(i):
        return remote(piece(0, i), piece(2, i), ex_s.at[1, i], ex_r.at[1, i], dev(sp, far))

    def on(i):
        return remote(piece(2, i), piece(3, i), ex_s.at[2, i], ex_r.at[2, i], dev(sp, sib))

    def send(*chunks):
        for i in chunks:
            to_far(i).start()
            to_sib(i).start()

    lane = lax.broadcasted_iota(jnp.int32, (8, T), 1)
    low_iota = lax.broadcasted_iota(jnp.int32, (T, T), 0)
    sub = lax.broadcasted_iota(jnp.int32, (8, T), 0)
    nothing = jnp.zeros((8, T), F32)

    def trees(row_lo, row_hi):
        def step(g, r):
            start = r * C + g * GROUP
            for q in range(GROUP // 8):
                rows = pl.ds(pl.multiple_of(start + q * 8, 8), 8)
                ids = species[rows, :]
                live = lane < cnt_b[rows, :]
                high = jnp.where(live, lax.shift_right_arithmetic(ids, 7) - 4 * me, -1)
                low = ids & 127
                value = growth[rows, :].astype(BF).astype(F32)

                def left_side(p):
                    chosen = jnp.broadcast_to(high[p : p + 1, :], (8, T)) == (sub & 3)
                    held_value = jnp.where(sub < 4, jnp.broadcast_to(value[p : p + 1, :], (8, T)), 1.0)
                    return jnp.where(chosen, held_value, 0.0)

                def right_side(p):
                    same = jnp.broadcast_to(low[p : p + 1, :], (T, T)) == low_iota
                    return jnp.where(same, 1.0, 0.0).astype(BF)

                for p in range(0, 8, 2):
                    a = jnp.concatenate(
                        [
                            jnp.concatenate([left_side(p), nothing], 1),
                            jnp.concatenate([nothing, left_side(p + 1)], 1),
                        ],
                        0,
                    ).astype(BF)
                    b = jnp.concatenate([right_side(p), right_side(p + 1)], 1)
                    both = lax.dot_general(a, b, (((1,), (1,)), ((), ())), preferred_element_type=F32)
                    for j in range(2):
                        sums[pl.ds(g * GROUP + q * 8 + p + j, 8, stride=C), :] = both[j * 8 : (j + 1) * 8, :]
            return r

        def whole(r, carry):
            lax.fori_loop(0, C // GROUP, step, r)
            rows = pl.ds(pl.multiple_of(r * C, C), C)
            for h in range(4):
                cs = slice(h * T, (h + 1) * T)
                total = sums[h * C : (h + 1) * C, :]
                tally = sums[(h + 4) * C : (h + 5) * C, :]
                out[rows, cs] = noise[:, cs] * (total - tally * eff[rows, cs])
            return carry

        lax.fori_loop(row_lo, row_hi, whole, 0)

    def prior(ks, start, size, steps):
        def body(i, carry):
            rows = pl.ds(pl.multiple_of(start + i * size, 256), size)
            total = None
            for k in ks:
                q = prec[pl.ds(pl.multiple_of(block(k) * W, W), W), :]
                term = jnp.dot(spat[k, rows, :], q, preferred_element_type=F32)
                total = term if total is None else total + term
            out[rows, :] = out[rows, :] - total
            return carry

        lax.fori_loop(0, steps, body, 0)

    def store(i, start, size):
        rows = pl.ds(start, size)
        return pltpu.make_async_copy(out.at[rows], out_hbm.at[rows], out_sem.at[i])

    def gram_block(k):
        def body(i, carry):
            cs = pl.ds(pl.multiple_of(i * 256, 256), 256)
            part[k, :, cs] = jnp.dot(eff_t[...], spat[k, :, cs], preferred_element_type=F32).astype(BF)
            return carry

        lax.fori_loop(0, W // 256, body, 0)

    def gram_early(k):
        def body(i, carry):
            cs = pl.ds(pl.multiple_of(i * 256, 256), 256)
            late[k - 2, :, cs] = jnp.dot(
                eff_t[:, C : 5 * C], spat[k, C : 5 * C, cs], preferred_element_type=F32
            )
            return carry

        lax.fori_loop(0, W // 256, body, 0)

    def gram_late(k):
        def body(i, carry):
            cs = pl.ds(pl.multiple_of(i * 256, 256), 256)
            total = late[k - 2, :, cs]
            total = total + jnp.dot(eff_t[:, 0:C], spat[k, 0:C, cs], preferred_element_type=F32)
            total = total + jnp.dot(eff_t[:, 5 * C :], spat[k, 5 * C :, cs], preferred_element_type=F32)
            part[k, :, cs] = total.astype(BF)
            return carry

        lax.fori_loop(0, W // 256, body, 0)

    def z_peer(d):
        return dev(at(y, xh, (z + d) % 4), me)

    def gz(k, d):
        src = part.at[k, pl.ds(pl.multiple_of(((z + d) % 4) * 64, 64), 64)]
        return remote(src, rz.at[d - 1, k], gz_s.at[k, d - 1], gz_r.at[k, d - 1], z_peer(d))

    def gy(k):
        d = (block(k) - y + 4) % 4
        slot = (d + 3) % 4
        return remote(part.at[k, pl.ds(256, 256)], ry.at[slot], gy_s.at[k], gy_r.at[slot], dev(at(block(k), xh, z), me))

    def gram_send(k):
        for d in (1, 2, 3):
            gz(k, d).start()

        @pl.when(block(k) != y)
        def _():
            gy(k).start()

    def g2y(k):
        d = (block(k) - y + 4) % 4
        slot = (d + 3) % 4
        return remote(mid0.at[k], ry2.at[slot], g2y_s.at[k], g2y_r.at[slot], dev(at(block(k), xh, z), me))

    def g2z(d):
        src = mid1.at[pl.ds(pl.multiple_of(((z + d) % 4) * 64, 64), 64)]
        return remote(src, rz2.at[d - 1], g2z_s.at[d - 1], g2z_r.at[d - 1], z_peer(d))

    for r in (1, 2, 3, 4):
        first_row(r)
    spat_row(2)
    spat_row(3)
    send(0)
    tmp[0:R, :] = counts[...].astype(F32)
    cnt_cols = tmp[...].T
    for r in range(R):
        cnt_b[r * C : (r + 1) * C, :] = jnp.broadcast_to(cnt_cols[:, r : r + 1], (C, T)).astype(jnp.int32)
    load_species.wait()
    load_growth.wait()
    trees(0, 2)

    for i in range(4):
        halos[i].wait_recv()
    tmp[0:1, :] = kap_up[R - 1 : R, :]
    tmp[1:2, :] = kap_dn[0:1, :]
    kap_edge = tmp[...].T
    kap_b[0] = jnp.broadcast_to(kap_edge[:, 0:1], (C, T)) + 4.0
    kap_b[R + 1] = jnp.broadcast_to(kap_edge[:, 1:2], (C, T)) + 4.0

    @pl.when(sp == 0)
    def _():
        near[0] = jnp.zeros((C, W), F32)

    @pl.when(sp == 31)
    def _():
        near[1] = jnp.zeros((C, W), F32)

    first_row(0)
    first_row(5)
    spat_row(1)
    spat_row(4)
    send(1, 2)
    trees(2, 4)

    halos[4].wait_recv()
    halos[5].wait_recv()
    first_row(-1)
    first_row(6)

    @pl.when(sp == 0)
    def _():
        first[0] = jnp.zeros((C, W), F32)

    @pl.when(sp == 31)
    def _():
        first[R + 1] = jnp.zeros((C, W), F32)

    spat_row(0)
    spat_row(5)
    send(3, 4)

    to_far(0).wait_recv()
    on(0).start()

    for r in range(R):
        eff_t[:, r * C : (r + 1) * C] = eff[r * C : (r + 1) * C, :].T.astype(BF)
    gram_block(0)
    gram_send(0)
    for i in range(5):
        to_sib(i).wait_recv()
    gram_block(1)
    gram_send(1)
    trees(4, 6)
    load_prec.wait()
    prior((0, 1), 0, 512, 3)

    for i in (1, 2):
        to_far(i).wait_recv()
        on(i).start()
    gram_early(2)
    for i in (0, 1, 2):
        on(i).wait_recv()
    gram_early(3)
    prior((2, 3), C, 512, 2)
    store(0, C, 4 * C).start()

    for i in (3, 4):
        to_far(i).wait_recv()
        on(i).start()
    gram_late(2)
    gram_send(2)
    for i in (3, 4):
        on(i).wait_recv()
    gram_late(3)
    gram_send(3)
    prior((2, 3), 0, C, 1)
    prior((2, 3), 5 * C, C, 1)
    store(1, 0, C).start()
    store(2, 5 * C, C).start()

    own_rows = pl.ds(pl.multiple_of(z * 64, 64), 64)
    for k in range(4):
        for d in (1, 2, 3):
            gz(k, d).wait_recv()
        total = part[k, own_rows, :].astype(F32)
        for d in (1, 2, 3):
            total = total + rz[d - 1, k].astype(F32)
        mid0[k] = total.astype(BF)

        @pl.when(block(k) != y)
        def _():
            g2y(k).start()

    for slot in range(3):
        remote(ry.at[slot], ry.at[slot], gy_s.at[0], gy_r.at[slot], dev(sp, sib)).wait_recv()
    for q in range(4):
        rows = slice(q * 64, (q + 1) * 64)
        total = part[mine, 256 + q * 64 : 256 + (q + 1) * 64, :].astype(F32)
        for slot in range(3):
            total = total + ry[slot, rows, :].astype(F32)
        mid1[rows, :] = total.astype(BF)
    for d in (1, 2, 3):
        g2z(d).start()

    for slot in range(3):
        remote(ry2.at[slot], ry2.at[slot], g2y_s.at[0], g2y_r.at[slot], dev(sp, sib)).wait_recv()
    total = mid0[mine].astype(F32)
    for slot in range(3):
        total = total + ry2[slot].astype(F32)
    held[0] = total
    for d in (1, 2, 3):
        g2z(d).wait_recv()
    total = mid1[own_rows, :].astype(F32)
    for d in (1, 2, 3):
        total = total + rz2[d - 1].astype(F32)
    held[1] = total

    def to_result(h, i, to_slot):
        return remote(held.at[h], fin.at[to_slot], last_s.at[i], last_r.at[to_slot], dev(at(me, h, z), y))

    to_result(1 - xh, 0, xh).start()

    @pl.when(moved)
    def _():
        to_result(xh, 1, xh).start()

    @pl.when(jnp.logical_not(moved))
    def _():
        fin[xh] = held[xh]

    remote(held.at[0], fin.at[1 - xh], last_s.at[0], last_r.at[1 - xh], dev(sp, sib)).wait_recv()

    @pl.when(moved)
    def _():
        remote(held.at[0], fin.at[xh], last_s.at[1], last_r.at[xh], dev(sp, sib)).wait_recv()

    gram[...] = (fin[0] + fin[1]) * (-0.5 / (NP * 32))

    for copy in halos:
        copy.wait_send()
    for i in range(5):
        to_sib(i).wait_send()
        to_far(i).wait_send()
        on(i).wait_send()
    for k in range(4):
        for d in (1, 2, 3):
            gz(k, d).wait_send()

        @pl.when(block(k) != y)
        def _():
            gy(k).wait_send()
            g2y(k).wait_send()

    for d in (1, 2, 3):
        g2z(d).wait_send()
    to_result(1 - xh, 0, xh).wait_send()

    @pl.when(moved)
    def _():
        to_result(xh, 1, xh).wait_send()

    store(0, C, 4 * C).wait()
    store(1, 0, C).wait()
    store(2, 5 * C, C).wait()


def finish(grad_in, gram_in, grad_out, gram_out, grad, gram, sem_in, sem_out):
    grad_rows = [pl.ds(r * C, C) for r in range(R)]
    loads = [pltpu.make_async_copy(grad_in.at[rows], grad.at[rows], sem_in.at[r]) for r, rows in enumerate(grad_rows)]
    loads.append(pltpu.make_async_copy(gram_in, gram, sem_in.at[R]))
    stores = [pltpu.make_async_copy(grad.at[rows], grad_out.at[rows], sem_out.at[r]) for r, rows in enumerate(grad_rows)]
    stores.append(pltpu.make_async_copy(gram, gram_out, sem_out.at[R]))
    for load in loads:
        load.start()
    for load, store in zip(loads, stores):
        load.wait()
        store.start()
    for store in stores:
        store.wait()


def shards(effects, kappa_sq, growth, tree_species, tree_counts, noise_precision, species_precision):
    vmem = pl.BlockSpec(memory_space=pltpu.VMEM)
    hbm = pl.BlockSpec(memory_space=pl.ANY)
    dma = pltpu.SemaphoreType.DMA
    grad, gram = pl.pallas_call(
        kernel,
        out_shape=(jax.ShapeDtypeStruct((NP, W), F32), jax.ShapeDtypeStruct((64, W), F32)),
        in_specs=[hbm, vmem, hbm, hbm, vmem, vmem, hbm],
        out_specs=(hbm, vmem),
        scratch_shapes=[
            pltpu.VMEM((NP, W), F32),
            pltpu.VMEM((NP, T), F32),
            pltpu.VMEM((NP, T), jnp.int32),
            pltpu.VMEM((4 * W, W), BF),
            pltpu.VMEM((NP, W), F32),
            pltpu.VMEM((2, C, W), F32),
            pltpu.VMEM((2, C, W), BF),
            pltpu.VMEM((2, C, W), BF),
            pltpu.VMEM((R, C), F32),
            pltpu.VMEM((R, C), F32),
            pltpu.VMEM((8, C), F32),
            pltpu.VMEM((R + 2, C, T), F32),
            pltpu.VMEM((NP, T), jnp.int32),
            pltpu.VMEM((R + 2, C, W), F32),
            pltpu.VMEM((4, NP, W), BF),
            pltpu.VMEM((W, NP), BF),
            pltpu.VMEM((8 * C, T), F32),
            pltpu.VMEM((4, W, W), BF),
            pltpu.VMEM((2, W, W), F32),
            pltpu.VMEM((3, 4, 64, W), BF),
            pltpu.VMEM((3, 256, W), BF),
            pltpu.VMEM((4, 64, W), BF),
            pltpu.VMEM((256, W), BF),
            pltpu.VMEM((3, 64, W), BF),
            pltpu.VMEM((3, 64, W), BF),
            pltpu.VMEM((2, 64, W), F32),
            pltpu.VMEM((2, 64, W), F32),
            dma((6,)), dma((6,)),
            dma((3, 5)), dma((3, 5)),
            dma((4, 3)), dma((4, 3)),
            dma((4,)), dma((3,)),
            dma((4,)), dma((3,)),
            dma((3,)), dma((3,)),
            dma((2,)), dma((2,)),
            dma((R + 3,)),
            dma((3,)),
        ],
        compiler_params=pltpu.CompilerParams(
            collective_id=0, has_side_effects=True, vmem_limit_bytes=56 << 20
        ),
        cost_estimate=pl.CostEstimate(flops=7_000_000_000, bytes_accessed=12_000_000, transcendentals=0),
        name="posterior_gradient",
    )(
        effects.reshape(NP, W),
        kappa_sq,
        growth.reshape(NP, T),
        tree_species.reshape(NP, T),
        tree_counts,
        noise_precision.reshape(1, W),
        species_precision,
    )
    grad, gram = pl.pallas_call(
        finish,
        out_shape=(jax.ShapeDtypeStruct((NP, W), F32), jax.ShapeDtypeStruct((64, W), F32)),
        in_specs=[hbm, hbm],
        out_specs=(hbm, hbm),
        scratch_shapes=[pltpu.VMEM((NP, W), F32), pltpu.VMEM((64, W), F32), dma((R + 1,)), dma((R + 1,))],
        compiler_params=pltpu.CompilerParams(vmem_limit_bytes=56 << 20),
        name="finish",
    )(grad, gram)
    return grad.reshape(R, C, W), gram


def solution(mesh):
    return jax.shard_map(
        shards,
        mesh=mesh,
        in_specs=(
            P("space", None, "species"),
            P("space", None),
            P("space", None, None),
            P("space", None, None),
            P("space", None),
            P("species"),
            P(None, "species"),
        ),
        out_specs=(P("space", None, "species"), P("space", "species")),
        check_vma=False,
    )
```

```python
import jax
import jax.numpy as jnp
from jax import lax
from jax.experimental import pallas as pl
from jax.experimental.pallas import tpu as pltpu
from jax.sharding import PartitionSpec as P

MESH = pl.DeviceIdType.MESH
BF = jnp.bfloat16
F32 = jnp.float32
R, C, W, T = 6, 256, 512, 128
NP = R * C
GROUP = 32
CHUNKS = ((2, 2), (1, 1), (4, 1), (0, 1), (5, 1))


def kernel(
    eff_in, kap, growth_in, species_in, counts, noise, prec_in,
    out_hbm, gram,
    eff, growth, species, prec, out,
    near, far_out, far_in, relay, kap_up, kap_dn, tmp, kap_b, cnt_b, first, spat, eff_t, sums,
    part, late, rz, ry, mid0, mid1, rz2, ry2, held, fin,
    halo_s, halo_r, ex_s, ex_r, gz_s, gz_r, gy_s, gy_r, g2y_s, g2y_r, g2z_s, g2z_r, last_s, last_r, in_sem, out_sem,
):
    sp, me = lax.axis_index("space"), lax.axis_index("species")
    z, xh, y = sp % 4, (sp // 4) % 2, sp // 8
    up, dn = (sp + 31) % 32, (sp + 1) % 32
    sib = (me // 2) * 2 + (me + 1) % 2
    far = (me + 2) % 4

    def at(yy, hh, zz):
        return (yy * 2 + hh) * 4 + zz

    def dev(space, spec):
        return {"space": space, "species": spec}

    def block(k):
        return ((me // 2 + k // 2) % 2) * 2 + (me % 2 + k % 2) % 2

    moved = y != me

    def remote(src, dst, ssem, rsem, to):
        return pltpu.make_async_remote_copy(
            src_ref=src, dst_ref=dst, send_sem=ssem, recv_sem=rsem, device_id=to, device_id_type=MESH
        )

    barrier = pltpu.get_barrier_semaphore()
    peers = [dev(up, me), dev(dn, me), dev(sp, sib), dev(sp, far)]
    peers += [dev(at(y, xh, (z + d) % 4), me) for d in (1, 2, 3)]
    peers += [dev(at((y + d) % 4, xh, z), me) for d in (1, 2, 3)]
    peers += [dev(at((y + d) % 4, h, z), y) for d in (1, 2, 3) for h in (0, 1)]
    peers += [dev(at(y, 1 - xh, z), y)]
    for peer in peers:
        pl.semaphore_signal(barrier, inc=1, device_id=peer, device_id_type=MESH)

    @pl.when(moved)
    def _():
        pl.semaphore_signal(barrier, inc=1, device_id=dev(sp, y), device_id_type=MESH)

    @pl.when(z == 0)
    def _():
        pl.semaphore_signal(barrier, inc=1, device_id=dev((sp + 30) % 32, me), device_id_type=MESH)

    @pl.when(z == 3)
    def _():
        pl.semaphore_signal(barrier, inc=1, device_id=dev((sp + 2) % 32, me), device_id_type=MESH)

    between = jnp.logical_or(z == 1, z == 2)

    loads = [pltpu.make_async_copy(eff_in.at[pl.ds(r * C, C)], eff.at[pl.ds(r * C, C)], in_sem.at[r]) for r in range(R)]
    for r in (1, 4, 2, 3, 0, 5):
        loads[r].start()
    load_species = pltpu.make_async_copy(species_in, species, in_sem.at[R])
    load_growth = pltpu.make_async_copy(growth_in, growth, in_sem.at[R + 1])
    load_prec = pltpu.make_async_copy(prec_in, prec, in_sem.at[R + 2])
    load_species.start()
    load_growth.start()
    load_prec.start()

    pl.semaphore_wait(barrier, len(peers) + moved.astype(jnp.int32) + between.astype(jnp.int32))

    def far_row(i):
        return remote(
            far_out.at[i], far_in.at[i], halo_s.at[4 + i], halo_r.at[4 + i], dev(up if i == 0 else dn, me)
        )

    halos = [
        remote(eff_in.at[pl.ds(0, C)], near.at[1], halo_s.at[0], halo_r.at[0], dev(up, me)),
        remote(eff_in.at[pl.ds(5 * C, C)], near.at[0], halo_s.at[1], halo_r.at[1], dev(dn, me)),
        remote(kap, kap_dn, halo_s.at[2], halo_r.at[2], dev(up, me)),
        remote(kap, kap_up, halo_s.at[3], halo_r.at[3], dev(dn, me)),
        far_row(0),
        far_row(1),
    ]
    for copy in halos[:4]:
        copy.start()
    crossing = (z == 0, z == 3)
    relayed = (z == 1, z == 2)

    def to_relay(i):
        return remote(far_out.at[i], relay, halo_s.at[4 + i], halo_r.at[6], dev(dn if i == 0 else up, me))

    def from_relay(i):
        to = (sp + 30) % 32 if i == 0 else (sp + 2) % 32
        return remote(relay, far_in.at[i], halo_s.at[6], halo_r.at[4 + i], dev(to, me))

    for i, r in enumerate((1, 4)):
        loads[r].wait()
        far_out[i] = eff[r * C : (r + 1) * C, :].astype(BF)

        @pl.when(crossing[i])
        def _():
            to_relay(i).start()

        @pl.when(jnp.logical_not(crossing[i]))
        def _():
            halos[4 + i].start()

    tmp[...] = jnp.zeros_like(tmp)
    tmp[0:R, :] = kap[...]
    kap_cols = tmp[...].T
    for r in range(R):
        kap_b[r + 1] = jnp.broadcast_to(kap_cols[:, r : r + 1], (C, T)) + 4.0

    for r in (2, 3, 0, 5):
        loads[r].wait()

    def erow(r):
        if 0 <= r < R:
            return eff.at[pl.ds(r * C, C)]
        return {-2: far_in.at[1], -1: near.at[0], 6: near.at[1], 7: far_in.at[0]}[r]

    edge = lax.broadcasted_iota(jnp.int32, (C, T), 0)

    def stencil(centre, above, below, kappa):
        left = jnp.where(edge == 0, 0.0, pltpu.roll(centre, 1, 0))
        right = jnp.where(edge == C - 1, 0.0, pltpu.roll(centre, C - 1, 0))
        return kappa * centre - (below + above + right + left)

    def first_row(r):
        def body(c, carry):
            cs = pl.ds(pl.multiple_of(c * T, T), T)
            first[r + 1, :, cs] = stencil(
                erow(r)[:, cs], erow(r - 1)[:, cs].astype(F32), erow(r + 1)[:, cs].astype(F32), kap_b[r + 1]
            )
            return carry

        lax.fori_loop(0, W // T, body, 0)

    def spat_row(r):
        def body(c, carry):
            cs = pl.ds(pl.multiple_of(c * T, T), T)
            s = stencil(first[r + 1, :, cs], first[r, :, cs], first[r + 2, :, cs], kap_b[r + 1])
            spat[0, r * C : (r + 1) * C, cs] = s.astype(BF)
            return carry

        lax.fori_loop(0, W // T, body, 0)

    def piece(k, i):
        r, n = CHUNKS[i]
        return spat.at[k, pl.ds(r * C, n * C)]

    def to_sib(i):
        return remote(piece(0, i), piece(1, i), ex_s.at[0, i], ex_r.at[0, i], dev(sp, sib))

    def to_far(i):
        return remote(piece(0, i), piece(2, i), ex_s.at[1, i], ex_r.at[1, i], dev(sp, far))

    def on(i):
        return remote(piece(2, i), piece(3, i), ex_s.at[2, i], ex_r.at[2, i], dev(sp, sib))

    def send(*chunks):
        for i in chunks:
            to_far(i).start()
            to_sib(i).start()

    lane = lax.broadcasted_iota(jnp.int32, (8, T), 1)
    low_iota = lax.broadcasted_iota(jnp.int32, (T, T), 0)
    sub = lax.broadcasted_iota(jnp.int32, (8, T), 0)
    nothing = jnp.zeros((8, T), F32)

    def trees(row_lo, row_hi):
        def step(g, r):
            start = r * C + g * GROUP
            for q in range(GROUP // 8):
                rows = pl.ds(pl.multiple_of(start + q * 8, 8), 8)
                ids = species[rows, :]
                live = lane < cnt_b[rows, :]
                high = jnp.where(live, lax.shift_right_arithmetic(ids, 7) - 4 * me, -1)
                low = ids & 127
                value = growth[rows, :].astype(BF).astype(F32)

                def left_side(p):
                    chosen = jnp.broadcast_to(high[p : p + 1, :], (8, T)) == (sub & 3)
                    held_value = jnp.where(sub < 4, jnp.broadcast_to(value[p : p + 1, :], (8, T)), 1.0)
                    return jnp.where(chosen, held_value, 0.0)

                def right_side(p):
                    same = jnp.broadcast_to(low[p : p + 1, :], (T, T)) == low_iota
                    return jnp.where(same, 1.0, 0.0).astype(BF)

                for p in range(0, 8, 2):
                    a = jnp.concatenate(
                        [
                            jnp.concatenate([left_side(p), nothing], 1),
                            jnp.concatenate([nothing, left_side(p + 1)], 1),
                        ],
                        0,
                    ).astype(BF)
                    b = jnp.concatenate([right_side(p), right_side(p + 1)], 1)
                    both = lax.dot_general(a, b, (((1,), (1,)), ((), ())), preferred_element_type=F32)
                    for j in range(2):
                        sums[pl.ds(g * GROUP + q * 8 + p + j, 8, stride=C), :] = both[j * 8 : (j + 1) * 8, :]
            return r

        def whole(r, carry):
            lax.fori_loop(0, C // GROUP, step, r)
            rows = pl.ds(pl.multiple_of(r * C, C), C)
            for h in range(4):
                cs = slice(h * T, (h + 1) * T)
                total = sums[h * C : (h + 1) * C, :]
                tally = sums[(h + 4) * C : (h + 5) * C, :]
                out[rows, cs] = noise[:, cs] * (total - tally * eff[rows, cs])
            return carry

        lax.fori_loop(row_lo, row_hi, whole, 0)

    def prior(ks, start, size, steps):
        def body(i, carry):
            rows = pl.ds(pl.multiple_of(start + i * size, 256), size)
            total = None
            for k in ks:
                q = prec[pl.ds(pl.multiple_of(block(k) * W, W), W), :]
                term = jnp.dot(spat[k, rows, :], q, preferred_element_type=F32)
                total = term if total is None else total + term
            out[rows, :] = out[rows, :] - total
            return carry

        lax.fori_loop(0, steps, body, 0)

    def store(i, start, size):
        rows = pl.ds(start, size)
        return pltpu.make_async_copy(out.at[rows], out_hbm.at[rows], out_sem.at[i])

    def gram_block(k):
        def body(i, carry):
            cs = pl.ds(pl.multiple_of(i * 256, 256), 256)
            part[k, :, cs] = jnp.dot(eff_t[...], spat[k, :, cs], preferred_element_type=F32).astype(BF)
            return carry

        lax.fori_loop(0, W // 256, body, 0)

    def gram_early(k):
        def body(i, carry):
            cs = pl.ds(pl.multiple_of(i * 256, 256), 256)
            late[k - 2, :, cs] = jnp.dot(
                eff_t[:, C : 5 * C], spat[k, C : 5 * C, cs], preferred_element_type=F32
            )
            return carry

        lax.fori_loop(0, W // 256, body, 0)

    def gram_late(k):
        def body(i, carry):
            cs = pl.ds(pl.multiple_of(i * 256, 256), 256)
            total = late[k - 2, :, cs]
            total = total + jnp.dot(eff_t[:, 0:C], spat[k, 0:C, cs], preferred_element_type=F32)
            total = total + jnp.dot(eff_t[:, 5 * C :], spat[k, 5 * C :, cs], preferred_element_type=F32)
            part[k, :, cs] = total.astype(BF)
            return carry

        lax.fori_loop(0, W // 256, body, 0)

    def z_peer(d):
        return dev(at(y, xh, (z + d) % 4), me)

    def gz(k, d):
        src = part.at[k, pl.ds(pl.multiple_of(((z + d) % 4) * 64, 64), 64)]
        return remote(src, rz.at[d - 1, k], gz_s.at[k, d - 1], gz_r.at[k, d - 1], z_peer(d))

    def y_peer(d):
        return dev(at((y + d) % 4, xh, z), me)

    def gy(k, d):
        src = part.at[k, pl.ds(256, 256), pl.ds(pl.multiple_of(((y + d) % 4) * T, T), T)]
        return remote(src, ry.at[d - 1, k], gy_s.at[k, d - 1], gy_r.at[k, d - 1], y_peer(d))

    def gram_send(k):
        for d in (1, 2, 3):
            gz(k, d).start()
            gy(k, d).start()

    def g2y(d):
        return remote(mid0.at[(y + d) % 4], ry2.at[d - 1], g2y_s.at[d - 1], g2y_r.at[d - 1], y_peer(d))

    def g2z(d):
        src = mid1.at[pl.ds(pl.multiple_of(((z + d) % 4) * 64, 64), 64)]
        return remote(src, rz2.at[d - 1], g2z_s.at[d - 1], g2z_r.at[d - 1], z_peer(d))

    for r in (1, 2, 3, 4):
        first_row(r)
    spat_row(2)
    spat_row(3)
    send(0)
    tmp[0:R, :] = counts[...].astype(F32)
    cnt_cols = tmp[...].T
    for r in range(R):
        cnt_b[r * C : (r + 1) * C, :] = jnp.broadcast_to(cnt_cols[:, r : r + 1], (C, T)).astype(jnp.int32)
    load_species.wait()
    load_growth.wait()
    trees(0, 2)
    for i in range(2):

        @pl.when(relayed[i])
        def _():
            to_relay(i).wait_recv()
            from_relay(i).start()

    for i in range(4):
        halos[i].wait_recv()
    tmp[0:1, :] = kap_up[R - 1 : R, :]
    tmp[1:2, :] = kap_dn[0:1, :]
    kap_edge = tmp[...].T
    kap_b[0] = jnp.broadcast_to(kap_edge[:, 0:1], (C, T)) + 4.0
    kap_b[R + 1] = jnp.broadcast_to(kap_edge[:, 1:2], (C, T)) + 4.0

    @pl.when(sp == 0)
    def _():
        near[0] = jnp.zeros((C, W), F32)

    @pl.when(sp == 31)
    def _():
        near[1] = jnp.zeros((C, W), F32)

    first_row(0)
    first_row(5)
    spat_row(1)
    spat_row(4)
    send(1, 2)
    trees(2, 4)

    halos[4].wait_recv()
    halos[5].wait_recv()
    first_row(-1)
    first_row(6)

    @pl.when(sp == 0)
    def _():
        first[0] = jnp.zeros((C, W), F32)

    @pl.when(sp == 31)
    def _():
        first[R + 1] = jnp.zeros((C, W), F32)

    spat_row(0)
    spat_row(5)
    send(3, 4)

    to_far(0).wait_recv()
    on(0).start()

    for r in range(R):
        eff_t[:, r * C : (r + 1) * C] = eff[r * C : (r + 1) * C, :].T.astype(BF)
    gram_block(0)
    gram_send(0)
    for i in range(5):
        to_sib(i).wait_recv()
    gram_block(1)
    gram_send(1)
    trees(4, 6)
    load_prec.wait()
    prior((0, 1), 0, 512, 3)

    for i in (1, 2):
        to_far(i).wait_recv()
        on(i).start()
    gram_early(2)
    for i in (0, 1, 2):
        on(i).wait_recv()
    gram_early(3)
    prior((2, 3), C, 512, 2)
    store(0, C, 4 * C).start()

    for i in (3, 4):
        to_far(i).wait_recv()
        on(i).start()
    gram_late(2)
    gram_send(2)
    for i in (3, 4):
        on(i).wait_recv()
    gram_late(3)
    gram_send(3)
    prior((2, 3), 0, C, 1)
    prior((2, 3), 5 * C, C, 1)
    store(1, 0, C).start()
    store(2, 5 * C, C).start()

    own_rows = pl.ds(pl.multiple_of(z * 64, 64), 64)
    own_cols = pl.ds(pl.multiple_of(y * T, T), T)
    for k in range(4):
        for d in (1, 2, 3):
            gz(k, d).wait_recv()
        total = part[k, own_rows, :].astype(F32)
        for d in (1, 2, 3):
            total = total + rz[d - 1, k].astype(F32)
        for q in range(4):
            mid0[q, :, k * T : (k + 1) * T] = total[:, q * T : (q + 1) * T].astype(BF)
    for d in (1, 2, 3):
        g2y(d).start()

    for k in range(4):
        for d in (1, 2, 3):
            gy(k, d).wait_recv()
        total = part[k, 256:512, own_cols].astype(F32)
        for d in (1, 2, 3):
            total = total + ry[d - 1, k].astype(F32)
        mid1[:, k * T : (k + 1) * T] = total.astype(BF)
    for d in (1, 2, 3):
        g2z(d).start()

    for d in (1, 2, 3):
        g2y(d).wait_recv()
    total = mid0[y].astype(F32)
    for d in (1, 2, 3):
        total = total + ry2[d - 1].astype(F32)
    held[0] = total
    for d in (1, 2, 3):
        g2z(d).wait_recv()
    total = mid1[own_rows, :].astype(F32)
    for d in (1, 2, 3):
        total = total + rz2[d - 1].astype(F32)
    held[1] = total

    def to_result(away, k):
        h = 1 - xh if away else xh
        return remote(
            held.at[h, :, pl.ds(k * T, T)],
            fin.at[xh, :, own_cols],
            last_s.at[away, k],
            last_r.at[xh, y],
            dev(at(me, h, z), block(k)),
        )

    def arrived(h, q):
        return remote(
            held.at[0, :, pl.ds(0, T)], fin.at[h, :, pl.ds(q * T, T)], last_s.at[0, 0], last_r.at[h, q], dev(sp, sib)
        )

    for k in (1, 2, 3):
        to_result(1, k).start()
        to_result(0, k).start()
    to_result(1, 0).start()

    @pl.when(moved)
    def _():
        to_result(0, 0).start()

    @pl.when(jnp.logical_not(moved))
    def _():
        fin[xh, :, own_cols] = held[xh, :, 0:T]

    for h in range(2):
        for q in range(4):

            @pl.when(jnp.logical_or(jnp.logical_or(h != xh, q != y), moved))
            def _():
                arrived(h, q).wait_recv()

    gram[...] = (fin[0] + fin[1]) * (-0.5 / (NP * 32))

    for copy in halos:
        copy.wait_send()
    for i in range(2):

        @pl.when(relayed[i])
        def _():
            from_relay(i).wait_send()

    for i in range(5):
        to_sib(i).wait_send()
        to_far(i).wait_send()
        on(i).wait_send()
    for d in (1, 2, 3):
        for k in range(4):
            gz(k, d).wait_send()
            gy(k, d).wait_send()
        g2y(d).wait_send()
        g2z(d).wait_send()
    for k in (1, 2, 3):
        to_result(1, k).wait_send()
        to_result(0, k).wait_send()
    to_result(1, 0).wait_send()

    @pl.when(moved)
    def _():
        to_result(0, 0).wait_send()

    store(0, C, 4 * C).wait()
    store(1, 0, C).wait()
    store(2, 5 * C, C).wait()


def finish(grad_in, gram_in, grad_out, gram_out, grad, gram, sem_in, sem_out):
    grad_rows = [pl.ds(r * C, C) for r in range(R)]
    loads = [pltpu.make_async_copy(grad_in.at[rows], grad.at[rows], sem_in.at[r]) for r, rows in enumerate(grad_rows)]
    loads.append(pltpu.make_async_copy(gram_in, gram, sem_in.at[R]))
    stores = [pltpu.make_async_copy(grad.at[rows], grad_out.at[rows], sem_out.at[r]) for r, rows in enumerate(grad_rows)]
    stores.append(pltpu.make_async_copy(gram, gram_out, sem_out.at[R]))
    for load in loads:
        load.start()
    for load, store in zip(loads, stores):
        load.wait()
        store.start()
    for store in stores:
        store.wait()


def shards(effects, kappa_sq, growth, tree_species, tree_counts, noise_precision, species_precision):
    vmem = pl.BlockSpec(memory_space=pltpu.VMEM)
    hbm = pl.BlockSpec(memory_space=pl.ANY)
    dma = pltpu.SemaphoreType.DMA
    grad, gram = pl.pallas_call(
        kernel,
        out_shape=(jax.ShapeDtypeStruct((NP, W), F32), jax.ShapeDtypeStruct((64, W), F32)),
        in_specs=[hbm, vmem, hbm, hbm, vmem, vmem, hbm],
        out_specs=(hbm, vmem),
        scratch_shapes=[
            pltpu.VMEM((NP, W), F32),
            pltpu.VMEM((NP, T), F32),
            pltpu.VMEM((NP, T), jnp.int32),
            pltpu.VMEM((4 * W, W), BF),
            pltpu.VMEM((NP, W), F32),
            pltpu.VMEM((2, C, W), F32),
            pltpu.VMEM((2, C, W), BF),
            pltpu.VMEM((2, C, W), BF),
            pltpu.VMEM((C, W), BF),
            pltpu.VMEM((R, C), F32),
            pltpu.VMEM((R, C), F32),
            pltpu.VMEM((8, C), F32),
            pltpu.VMEM((R + 2, C, T), F32),
            pltpu.VMEM((NP, T), jnp.int32),
            pltpu.VMEM((R + 2, C, W), F32),
            pltpu.VMEM((4, NP, W), BF),
            pltpu.VMEM((W, NP), BF),
            pltpu.VMEM((8 * C, T), F32),
            pltpu.VMEM((4, W, W), BF),
            pltpu.VMEM((2, W, W), F32),
            pltpu.VMEM((3, 4, 64, W), BF),
            pltpu.VMEM((3, 4, 256, T), BF),
            pltpu.VMEM((4, 64, W), BF),
            pltpu.VMEM((256, W), BF),
            pltpu.VMEM((3, 64, W), BF),
            pltpu.VMEM((3, 64, W), BF),
            pltpu.VMEM((2, 64, W), F32),
            pltpu.VMEM((2, 64, W), F32),
            dma((7,)), dma((7,)),
            dma((3, 5)), dma((3, 5)),
            dma((4, 3)), dma((4, 3)),
            dma((4, 3)), dma((4, 3)),
            dma((3,)), dma((3,)),
            dma((3,)), dma((3,)),
            dma((2, 4)), dma((2, 4)),
            dma((R + 3,)),
            dma((3,)),
        ],
        compiler_params=pltpu.CompilerParams(
            collective_id=0, has_side_effects=True, vmem_limit_bytes=56 << 20
        ),
        cost_estimate=pl.CostEstimate(flops=7_000_000_000, bytes_accessed=12_000_000, transcendentals=0),
        name="posterior_gradient",
    )(
        effects.reshape(NP, W),
        kappa_sq,
        growth.reshape(NP, T),
        tree_species.reshape(NP, T),
        tree_counts,
        noise_precision.reshape(1, W),
        species_precision,
    )
    grad, gram = pl.pallas_call(
        finish,
        out_shape=(jax.ShapeDtypeStruct((NP, W), F32), jax.ShapeDtypeStruct((64, W), F32)),
        in_specs=[hbm, hbm],
        out_specs=(hbm, hbm),
        scratch_shapes=[pltpu.VMEM((NP, W), F32), pltpu.VMEM((64, W), F32), dma((R + 1,)), dma((R + 1,))],
        compiler_params=pltpu.CompilerParams(vmem_limit_bytes=56 << 20),
        name="finish",
    )(grad, gram)
    return grad.reshape(R, C, W), gram


def solution(mesh):
    return jax.shard_map(
        shards,
        mesh=mesh,
        in_specs=(
            P("space", None, "species"),
            P("space", None),
            P("space", None, None),
            P("space", None, None),
            P("space", None),
            P("species"),
            P(None, "species"),
        ),
        out_specs=(P("space", None, "species"), P("space", "species")),
        check_vma=False,
    )
```

```python
import jax
import jax.numpy as jnp
from jax import lax
from jax.experimental import pallas as pl
from jax.experimental.pallas import tpu as pltpu
from jax.sharding import PartitionSpec as P

MESH = pl.DeviceIdType.MESH
BF = jnp.bfloat16
F32 = jnp.float32
R, C, W, T = 6, 256, 512, 128
NP = R * C
GROUP = 32
CHUNKS = ((2 * C, C // 2), (2 * C + C // 2, C // 2), (3 * C, C), (C, C), (4 * C, C), (0, C), (5 * C, C))
NC = len(CHUNKS)


def kernel(
    eff_in, kap, growth_in, species_in, counts, noise, prec_in,
    out_hbm, gram,
    eff, growth, species, prec, out,
    near, far_out, far_in, relayed, kap_up, kap_dn, tmp, kap_b, cnt_b, first, spat, eff_t, sums,
    part, late, rz, ry, mid0, mid1, rz2, ry2, held, fin,
    halo_s, halo_r, relay_s, relay_r, ex_s, ex_r, gz_s, gz_r, gy_s, gy_r, g2y_s, g2y_r, g2z_s, g2z_r, last_s, last_r, in_sem, out_sem,
):
    sp, me = lax.axis_index("space"), lax.axis_index("species")
    z, xh, y = sp % 4, (sp // 4) % 2, sp // 8
    up, dn = (sp + 31) % 32, (sp + 1) % 32
    sib = (me // 2) * 2 + (me + 1) % 2
    far = (me + 2) % 4

    def at(yy, hh, zz):
        return (yy * 2 + hh) * 4 + zz

    def dev(space, spec):
        return {"space": space, "species": spec}

    def block(k):
        return ((me // 2 + k // 2) % 2) * 2 + (me % 2 + k % 2) % 2

    moved = y != me

    def remote(src, dst, ssem, rsem, to):
        return pltpu.make_async_remote_copy(
            src_ref=src, dst_ref=dst, send_sem=ssem, recv_sem=rsem, device_id=to, device_id_type=MESH
        )

    barrier = pltpu.get_barrier_semaphore()
    peers = [dev(up, me), dev(dn, me), dev(sp, sib), dev(sp, far)]
    peers += [dev(at(y, xh, (z + d) % 4), me) for d in (1, 2, 3)]
    peers += [dev(at((y + d) % 4, xh, z), me) for d in (1, 2, 3)]
    peers += [dev(at((y + d) % 4, h, z), y) for d in (1, 2, 3) for h in (0, 1)]
    peers += [dev(at(y, 1 - xh, z), y)]
    for peer in peers:
        pl.semaphore_signal(barrier, inc=1, device_id=peer, device_id_type=MESH)

    @pl.when(moved)
    def _():
        pl.semaphore_signal(barrier, inc=1, device_id=dev(sp, y), device_id_type=MESH)

    outer = (z == 0, z == 3)
    inner = (z == 1, z == 2)
    for i in range(2):

        @pl.when(outer[i])
        def _():
            pl.semaphore_signal(barrier, inc=1, device_id=dev((dn, up)[i], far), device_id_type=MESH)

    is_inner = jnp.logical_or(z == 1, z == 2)

    loads = [pltpu.make_async_copy(eff_in.at[pl.ds(r * C, C)], eff.at[pl.ds(r * C, C)], in_sem.at[r]) for r in range(R)]
    for r in (1, 4, 2, 3, 0, 5):
        loads[r].start()
    load_species = pltpu.make_async_copy(species_in, species, in_sem.at[R])
    load_growth = pltpu.make_async_copy(growth_in, growth, in_sem.at[R + 1])
    load_prec = pltpu.make_async_copy(prec_in, prec, in_sem.at[R + 2])
    load_species.start()
    load_growth.start()
    load_prec.start()

    pl.semaphore_wait(barrier, len(peers) + moved.astype(jnp.int32) + is_inner.astype(jnp.int32))

    def far_row(i):
        return remote(
            far_out.at[i], far_in.at[i], halo_s.at[4 + i], halo_r.at[4 + i], dev(up if i == 0 else dn, me)
        )

    halos = [
        remote(eff_in.at[pl.ds(0, C)], near.at[1], halo_s.at[0], halo_r.at[0], dev(up, me)),
        remote(eff_in.at[pl.ds(5 * C, C)], near.at[0], halo_s.at[1], halo_r.at[1], dev(dn, me)),
        remote(kap, kap_dn, halo_s.at[2], halo_r.at[2], dev(up, me)),
        remote(kap, kap_up, halo_s.at[3], halo_r.at[3], dev(dn, me)),
        far_row(0),
        far_row(1),
    ]
    for copy in halos[:4]:
        copy.start()
    for i, r in enumerate((1, 4)):
        loads[r].wait()
        far_out[i] = eff[r * C : (r + 1) * C, :].astype(BF)
        halos[4 + i].start()

    tmp[...] = jnp.zeros_like(tmp)
    tmp[0:R, :] = kap[...]
    kap_cols = tmp[...].T
    for r in range(R):
        kap_b[r + 1] = jnp.broadcast_to(kap_cols[:, r : r + 1], (C, T)) + 4.0

    for r in (2, 3, 0, 5):
        loads[r].wait()

    def erow(r):
        if 0 <= r < R:
            return eff.at[pl.ds(r * C, C)]
        return {-2: far_in.at[1], -1: near.at[0], 6: near.at[1], 7: far_in.at[0]}[r]

    edge = lax.broadcasted_iota(jnp.int32, (C, T), 0)

    def stencil(centre, above, below, kappa):
        left = jnp.where(edge == 0, 0.0, pltpu.roll(centre, 1, 0))
        right = jnp.where(edge == C - 1, 0.0, pltpu.roll(centre, C - 1, 0))
        return kappa * centre - (below + above + right + left)

    def first_row(r):
        def body(c, carry):
            cs = pl.ds(pl.multiple_of(c * T, T), T)
            first[r + 1, :, cs] = stencil(
                erow(r)[:, cs], erow(r - 1)[:, cs].astype(F32), erow(r + 1)[:, cs].astype(F32), kap_b[r + 1]
            )
            return carry

        lax.fori_loop(0, W // T, body, 0)

    def spat_row(r):
        def body(c, carry):
            cs = pl.ds(pl.multiple_of(c * T, T), T)
            s = stencil(first[r + 1, :, cs], first[r, :, cs], first[r + 2, :, cs], kap_b[r + 1])
            spat[0, r * C : (r + 1) * C, cs] = s.astype(BF)
            return carry

        lax.fori_loop(0, W // T, body, 0)

    def piece(k, i):
        return spat.at[k, pl.ds(*CHUNKS[i])]

    def to_sib(i):
        return remote(piece(0, i), piece(1, i), ex_s.at[0, i], ex_r.at[0, i], dev(sp, sib))

    def to_far(i):
        return remote(piece(0, i), piece(2, i), ex_s.at[1, i], ex_r.at[1, i], dev(sp, far))

    def on(i):
        return remote(piece(2, i), piece(3, i), ex_s.at[2, i], ex_r.at[2, i], dev(sp, sib))

    def relay(j):
        return relayed.at[pl.ds(CHUNKS[j][0] - 2 * C, CHUNKS[j][1])]

    def to_relay(i, j):
        return remote(piece(0, j), relay(j), ex_s.at[1, j], relay_r.at[j], dev((dn, up)[i], me))

    def from_relay(i, j):
        return remote(relay(j), piece(2, j), relay_s.at[j], ex_r.at[1, j], dev((up, dn)[i], far))

    def pass_on(j):
        for i in range(2):

            @pl.when(inner[i])
            def _():
                to_relay(i, j).wait_recv()
                from_relay(i, j).start()

    def send(*chunks):
        for i in chunks:
            if i < 2:
                for t in range(2):

                    @pl.when(outer[t])
                    def _():
                        to_relay(t, i).start()

                @pl.when(is_inner)
                def _():
                    to_far(i).start()

            else:
                to_far(i).start()
            to_sib(i).start()

    lane = lax.broadcasted_iota(jnp.int32, (8, T), 1)
    low_iota = lax.broadcasted_iota(jnp.int32, (T, T), 0)
    sub = lax.broadcasted_iota(jnp.int32, (8, T), 0)
    nothing = jnp.zeros((8, T), F32)

    def trees(row_lo, row_hi):
        def step(g, r):
            start = r * C + g * GROUP
            for q in range(GROUP // 8):
                rows = pl.ds(pl.multiple_of(start + q * 8, 8), 8)
                ids = species[rows, :]
                live = lane < cnt_b[rows, :]
                high = jnp.where(live, lax.shift_right_arithmetic(ids, 7) - 4 * me, -1)
                low = ids & 127
                value = growth[rows, :].astype(BF).astype(F32)

                def left_side(p):
                    chosen = jnp.broadcast_to(high[p : p + 1, :], (8, T)) == (sub & 3)
                    held_value = jnp.where(sub < 4, jnp.broadcast_to(value[p : p + 1, :], (8, T)), 1.0)
                    return jnp.where(chosen, held_value, 0.0)

                def right_side(p):
                    same = jnp.broadcast_to(low[p : p + 1, :], (T, T)) == low_iota
                    return jnp.where(same, 1.0, 0.0).astype(BF)

                for p in range(0, 8, 2):
                    a = jnp.concatenate(
                        [
                            jnp.concatenate([left_side(p), nothing], 1),
                            jnp.concatenate([nothing, left_side(p + 1)], 1),
                        ],
                        0,
                    ).astype(BF)
                    b = jnp.concatenate([right_side(p), right_side(p + 1)], 1)
                    both = lax.dot_general(a, b, (((1,), (1,)), ((), ())), preferred_element_type=F32)
                    for j in range(2):
                        sums[pl.ds(g * GROUP + q * 8 + p + j, 8, stride=C), :] = both[j * 8 : (j + 1) * 8, :]
            return r

        def whole(r, carry):
            lax.fori_loop(0, C // GROUP, step, r)
            rows = pl.ds(pl.multiple_of(r * C, C), C)
            for h in range(4):
                cs = slice(h * T, (h + 1) * T)
                total = sums[h * C : (h + 1) * C, :]
                tally = sums[(h + 4) * C : (h + 5) * C, :]
                out[rows, cs] = noise[:, cs] * (total - tally * eff[rows, cs])
            return carry

        lax.fori_loop(row_lo, row_hi, whole, 0)

    def prior(ks, start, size, steps):
        def body(i, carry):
            rows = pl.ds(pl.multiple_of(start + i * size, 256), size)
            total = None
            for k in ks:
                q = prec[pl.ds(pl.multiple_of(block(k) * W, W), W), :]
                term = jnp.dot(spat[k, rows, :], q, preferred_element_type=F32)
                total = term if total is None else total + term
            out[rows, :] = out[rows, :] - total
            return carry

        lax.fori_loop(0, steps, body, 0)

    def store(i, start, size):
        rows = pl.ds(start, size)
        return pltpu.make_async_copy(out.at[rows], out_hbm.at[rows], out_sem.at[i])

    def gram_block(k):
        def body(i, carry):
            cs = pl.ds(pl.multiple_of(i * 256, 256), 256)
            part[k, :, cs] = jnp.dot(eff_t[...], spat[k, :, cs], preferred_element_type=F32).astype(BF)
            return carry

        lax.fori_loop(0, W // 256, body, 0)

    def gram_rows(k, starts, size, cs):
        total = None
        for r in starts:
            rows = slice(r * C, (r + size) * C)
            term = jnp.dot(eff_t[:, rows], spat[k, rows, cs], preferred_element_type=F32)
            total = term if total is None else total + term
        return total

    def gram_early(k):
        def body(i, carry):
            cs = pl.ds(pl.multiple_of(i * 256, 256), 256)
            late[k - 2, :, cs] = gram_rows(k, (1, 4), 1, cs)
            return carry

        lax.fori_loop(0, W // 256, body, 0)

    def gram_late(k):
        def body(i, carry):
            cs = pl.ds(pl.multiple_of(i * 256, 256), 256)
            total = late[k - 2, :, cs] + gram_rows(k, (2,), 2, cs) + gram_rows(k, (0, 5), 1, cs)
            part[k, :, cs] = total.astype(BF)
            return carry

        lax.fori_loop(0, W // 256, body, 0)

    def z_peer(d):
        return dev(at(y, xh, (z + d) % 4), me)

    def gz(k, d):
        src = part.at[k, pl.ds(pl.multiple_of(((z + d) % 4) * 64, 64), 64)]
        return remote(src, rz.at[d - 1, k], gz_s.at[k, d - 1], gz_r.at[k, d - 1], z_peer(d))

    def y_peer(d):
        return dev(at((y + d) % 4, xh, z), me)

    def gy(k, d):
        src = part.at[k, pl.ds(256, 256), pl.ds(pl.multiple_of(((y + d) % 4) * T, T), T)]
        return remote(src, ry.at[d - 1, k], gy_s.at[k, d - 1], gy_r.at[k, d - 1], y_peer(d))

    def gram_send(k):
        for d in (1, 2, 3):
            gz(k, d).start()
            gy(k, d).start()

    def g2y(d):
        return remote(mid0.at[(y + d) % 4], ry2.at[d - 1], g2y_s.at[d - 1], g2y_r.at[d - 1], y_peer(d))

    def g2z(d):
        src = mid1.at[pl.ds(pl.multiple_of(((z + d) % 4) * 64, 64), 64)]
        return remote(src, rz2.at[d - 1], g2z_s.at[d - 1], g2z_r.at[d - 1], z_peer(d))

    for r in (1, 2, 3, 4):
        first_row(r)
    spat_row(2)
    spat_row(3)
    send(2, 0, 1)
    tmp[0:R, :] = counts[...].astype(F32)
    cnt_cols = tmp[...].T
    for r in range(R):
        cnt_b[r * C : (r + 1) * C, :] = jnp.broadcast_to(cnt_cols[:, r : r + 1], (C, T)).astype(jnp.int32)
    load_species.wait()
    load_growth.wait()
    trees(0, 2)

    for i in range(4):
        halos[i].wait_recv()
    tmp[0:1, :] = kap_up[R - 1 : R, :]
    tmp[1:2, :] = kap_dn[0:1, :]
    kap_edge = tmp[...].T
    kap_b[0] = jnp.broadcast_to(kap_edge[:, 0:1], (C, T)) + 4.0
    kap_b[R + 1] = jnp.broadcast_to(kap_edge[:, 1:2], (C, T)) + 4.0

    @pl.when(sp == 0)
    def _():
        near[0] = jnp.zeros((C, W), F32)

    @pl.when(sp == 31)
    def _():
        near[1] = jnp.zeros((C, W), F32)

    first_row(0)
    first_row(5)
    spat_row(1)
    spat_row(4)
    send(3, 4)
    trees(2, 3)
    pass_on(0)
    pass_on(1)
    trees(3, 4)

    halos[4].wait_recv()
    halos[5].wait_recv()
    first_row(-1)
    first_row(6)

    @pl.when(sp == 0)
    def _():
        first[0] = jnp.zeros((C, W), F32)

    @pl.when(sp == 31)
    def _():
        first[R + 1] = jnp.zeros((C, W), F32)

    spat_row(0)
    spat_row(5)
    send(5, 6)

    for r in range(R):
        eff_t[:, r * C : (r + 1) * C] = eff[r * C : (r + 1) * C, :].T.astype(BF)
    gram_block(0)
    gram_send(0)
    for i in range(NC):
        to_sib(i).wait_recv()
    gram_block(1)
    gram_send(1)
    trees(4, 6)
    load_prec.wait()
    prior((0, 1), 0, 512, 3)

    for i in (3, 4):
        to_far(i).wait_recv()
        on(i).start()
    gram_early(2)
    for i in (3, 4):
        on(i).wait_recv()
    gram_early(3)
    prior((2, 3), C, C, 1)
    prior((2, 3), 4 * C, C, 1)
    store(0, C, C).start()
    store(1, 4 * C, C).start()

    for i in (2, 5, 6, 0, 1):
        to_far(i).wait_recv()
        on(i).start()
    gram_late(2)
    gram_send(2)
    for i in (2, 5, 6, 0, 1):
        on(i).wait_recv()
    gram_late(3)
    gram_send(3)
    prior((2, 3), 2 * C, 2 * C, 1)
    prior((2, 3), 0, C, 1)
    prior((2, 3), 5 * C, C, 1)
    store(2, 2 * C, 2 * C).start()
    store(3, 0, C).start()
    store(4, 5 * C, C).start()

    own_rows = pl.ds(pl.multiple_of(z * 64, 64), 64)
    own_cols = pl.ds(pl.multiple_of(y * T, T), T)
    for k in range(4):
        for d in (1, 2, 3):
            gz(k, d).wait_recv()
        total = part[k, own_rows, :].astype(F32)
        for d in (1, 2, 3):
            total = total + rz[d - 1, k].astype(F32)
        for q in range(4):
            mid0[q, :, k * T : (k + 1) * T] = total[:, q * T : (q + 1) * T].astype(BF)
    for d in (1, 2, 3):
        g2y(d).start()

    for k in range(4):
        for d in (1, 2, 3):
            gy(k, d).wait_recv()
        total = part[k, 256:512, own_cols].astype(F32)
        for d in (1, 2, 3):
            total = total + ry[d - 1, k].astype(F32)
        mid1[:, k * T : (k + 1) * T] = total.astype(BF)
    for d in (1, 2, 3):
        g2z(d).start()

    for d in (1, 2, 3):
        g2y(d).wait_recv()
    total = mid0[y].astype(F32)
    for d in (1, 2, 3):
        total = total + ry2[d - 1].astype(F32)
    held[0] = total
    for d in (1, 2, 3):
        g2z(d).wait_recv()
    total = mid1[own_rows, :].astype(F32)
    for d in (1, 2, 3):
        total = total + rz2[d - 1].astype(F32)
    held[1] = total

    def to_result(away, k):
        h = 1 - xh if away else xh
        return remote(
            held.at[h, :, pl.ds(k * T, T)],
            fin.at[xh, :, own_cols],
            last_s.at[away, k],
            last_r.at[xh, y],
            dev(at(me, h, z), block(k)),
        )

    def arrived(h, q):
        return remote(
            held.at[0, :, pl.ds(0, T)], fin.at[h, :, pl.ds(q * T, T)], last_s.at[0, 0], last_r.at[h, q], dev(sp, sib)
        )

    for k in (1, 2, 3):
        to_result(1, k).start()
        to_result(0, k).start()
    to_result(1, 0).start()

    @pl.when(moved)
    def _():
        to_result(0, 0).start()

    @pl.when(jnp.logical_not(moved))
    def _():
        fin[xh, :, own_cols] = held[xh, :, 0:T]

    for h in range(2):
        for q in range(4):

            @pl.when(jnp.logical_or(jnp.logical_or(h != xh, q != y), moved))
            def _():
                arrived(h, q).wait_recv()

    gram[...] = (fin[0] + fin[1]) * (-0.5 / (NP * 32))

    for copy in halos:
        copy.wait_send()
    for i in range(NC):
        to_sib(i).wait_send()
        to_far(i).wait_send()
        on(i).wait_send()
    for j in range(2):

        @pl.when(is_inner)
        def _():
            from_relay(0, j).wait_send()

    for d in (1, 2, 3):
        for k in range(4):
            gz(k, d).wait_send()
            gy(k, d).wait_send()
        g2y(d).wait_send()
        g2z(d).wait_send()
    for k in (1, 2, 3):
        to_result(1, k).wait_send()
        to_result(0, k).wait_send()
    to_result(1, 0).wait_send()

    @pl.when(moved)
    def _():
        to_result(0, 0).wait_send()

    for i, (start, size) in enumerate(((C, C), (4 * C, C), (2 * C, 2 * C), (0, C), (5 * C, C))):
        store(i, start, size).wait()


def finish(grad_in, gram_in, grad_out, gram_out, grad, gram, sem_in, sem_out):
    grad_rows = [pl.ds(r * C, C) for r in range(R)]
    loads = [pltpu.make_async_copy(grad_in.at[rows], grad.at[rows], sem_in.at[r]) for r, rows in enumerate(grad_rows)]
    loads.append(pltpu.make_async_copy(gram_in, gram, sem_in.at[R]))
    stores = [pltpu.make_async_copy(grad.at[rows], grad_out.at[rows], sem_out.at[r]) for r, rows in enumerate(grad_rows)]
    stores.append(pltpu.make_async_copy(gram, gram_out, sem_out.at[R]))
    for load in loads:
        load.start()
    for load, store in zip(loads, stores):
        load.wait()
        store.start()
    for store in stores:
        store.wait()


def shards(effects, kappa_sq, growth, tree_species, tree_counts, noise_precision, species_precision):
    vmem = pl.BlockSpec(memory_space=pltpu.VMEM)
    hbm = pl.BlockSpec(memory_space=pl.ANY)
    dma = pltpu.SemaphoreType.DMA
    grad, gram = pl.pallas_call(
        kernel,
        out_shape=(jax.ShapeDtypeStruct((NP, W), F32), jax.ShapeDtypeStruct((64, W), F32)),
        in_specs=[hbm, vmem, hbm, hbm, vmem, vmem, hbm],
        out_specs=(hbm, vmem),
        scratch_shapes=[
            pltpu.VMEM((NP, W), F32),
            pltpu.VMEM((NP, T), F32),
            pltpu.VMEM((NP, T), jnp.int32),
            pltpu.VMEM((4 * W, W), BF),
            pltpu.VMEM((NP, W), F32),
            pltpu.VMEM((2, C, W), F32),
            pltpu.VMEM((2, C, W), BF),
            pltpu.VMEM((2, C, W), BF),
            pltpu.VMEM((3 * C // 2, W), BF),
            pltpu.VMEM((R, C), F32),
            pltpu.VMEM((R, C), F32),
            pltpu.VMEM((8, C), F32),
            pltpu.VMEM((R + 2, C, T), F32),
            pltpu.VMEM((NP, T), jnp.int32),
            pltpu.VMEM((R + 2, C, W), F32),
            pltpu.VMEM((4, NP, W), BF),
            pltpu.VMEM((W, NP), BF),
            pltpu.VMEM((8 * C, T), F32),
            pltpu.VMEM((4, W, W), BF),
            pltpu.VMEM((2, W, W), F32),
            pltpu.VMEM((3, 4, 64, W), BF),
            pltpu.VMEM((3, 4, 256, T), BF),
            pltpu.VMEM((4, 64, W), BF),
            pltpu.VMEM((256, W), BF),
            pltpu.VMEM((3, 64, W), BF),
            pltpu.VMEM((3, 64, W), BF),
            pltpu.VMEM((2, 64, W), F32),
            pltpu.VMEM((2, 64, W), F32),
            dma((6,)), dma((6,)),
            dma((2,)), dma((2,)),
            dma((3, NC)), dma((3, NC)),
            dma((4, 3)), dma((4, 3)),
            dma((4, 3)), dma((4, 3)),
            dma((3,)), dma((3,)),
            dma((3,)), dma((3,)),
            dma((2, 4)), dma((2, 4)),
            dma((R + 3,)),
            dma((5,)),
        ],
        compiler_params=pltpu.CompilerParams(
            collective_id=0, has_side_effects=True, vmem_limit_bytes=56 << 20
        ),
        cost_estimate=pl.CostEstimate(flops=7_000_000_000, bytes_accessed=12_000_000, transcendentals=0),
        name="posterior_gradient",
    )(
        effects.reshape(NP, W),
        kappa_sq,
        growth.reshape(NP, T),
        tree_species.reshape(NP, T),
        tree_counts,
        noise_precision.reshape(1, W),
        species_precision,
    )
    grad, gram = pl.pallas_call(
        finish,
        out_shape=(jax.ShapeDtypeStruct((NP, W), F32), jax.ShapeDtypeStruct((64, W), F32)),
        in_specs=[hbm, hbm],
        out_specs=(hbm, hbm),
        scratch_shapes=[pltpu.VMEM((NP, W), F32), pltpu.VMEM((64, W), F32), dma((R + 1,)), dma((R + 1,))],
        compiler_params=pltpu.CompilerParams(vmem_limit_bytes=56 << 20),
        name="finish",
    )(grad, gram)
    return grad.reshape(R, C, W), gram


def solution(mesh):
    return jax.shard_map(
        shards,
        mesh=mesh,
        in_specs=(
            P("space", None, "species"),
            P("space", None),
            P("space", None, None),
            P("space", None, None),
            P("space", None),
            P("species"),
            P(None, "species"),
        ),
        out_specs=(P("space", None, "species"), P("space", "species")),
        check_vma=False,
    )
```

```python
import jax
import jax.numpy as jnp
from jax import lax
from jax.experimental import pallas as pl
from jax.experimental.pallas import tpu as pltpu
from jax.sharding import PartitionSpec as P

MESH = pl.DeviceIdType.MESH
BF = jnp.bfloat16
F32 = jnp.float32
R, C, W, T = 6, 256, 512, 128
NP = R * C
GROUP = 32
CHUNKS = ((2 * C, C // 2), (2 * C + C // 2, C // 2), (3 * C, C), (C, C), (4 * C, C), (0, C), (5 * C, C))
NC = len(CHUNKS)


def kernel(
    eff_in, kap, growth_in, species_in, counts, noise, prec_in,
    out_hbm, gram,
    eff, growth, species, prec, out,
    near, far_out, far_in, relayed, kap_up, kap_dn, tmp, kap_b, cnt_b, first, spat, eff_t, sums,
    part, late, rz, ry, mid0, mid1, rz2, ry2, held, fin,
    halo_s, halo_r, relay_s, relay_r, ex_s, ex_r, gz_s, gz_r, gy_s, gy_r, g2y_s, g2y_r, g2z_s, g2z_r, last_s, last_r, in_sem, out_sem,
):
    sp, me = lax.axis_index("space"), lax.axis_index("species")
    z, xh, y = sp % 4, (sp // 4) % 2, sp // 8
    up, dn = (sp + 31) % 32, (sp + 1) % 32
    sib = (me // 2) * 2 + (me + 1) % 2
    far = (me + 2) % 4

    def at(yy, hh, zz):
        return (yy * 2 + hh) * 4 + zz

    def dev(space, spec):
        return {"space": space, "species": spec}

    def block(k):
        return ((me // 2 + k // 2) % 2) * 2 + (me % 2 + k % 2) % 2

    moved = y != me

    def remote(src, dst, ssem, rsem, to):
        return pltpu.make_async_remote_copy(
            src_ref=src, dst_ref=dst, send_sem=ssem, recv_sem=rsem, device_id=to, device_id_type=MESH
        )

    barrier = pltpu.get_barrier_semaphore()
    peers = [dev(up, me), dev(dn, me), dev(sp, sib), dev(sp, far)]
    peers += [dev(at(y, xh, (z + d) % 4), me) for d in (1, 2, 3)]
    peers += [dev(at((y + d) % 4, xh, z), me) for d in (1, 2, 3)]
    peers += [dev(at((y + d) % 4, h, z), y) for d in (1, 2, 3) for h in (0, 1)]
    peers += [dev(at(y, 1 - xh, z), y)]
    for peer in peers:
        pl.semaphore_signal(barrier, inc=1, device_id=peer, device_id_type=MESH)

    @pl.when(moved)
    def _():
        pl.semaphore_signal(barrier, inc=1, device_id=dev(sp, y), device_id_type=MESH)

    outer = (z == 0, z == 3)
    inner = (z == 1, z == 2)
    for i in range(2):

        @pl.when(outer[i])
        def _():
            pl.semaphore_signal(barrier, inc=1, device_id=dev((dn, up)[i], far), device_id_type=MESH)

    is_inner = jnp.logical_or(z == 1, z == 2)

    loads = [pltpu.make_async_copy(eff_in.at[pl.ds(r * C, C)], eff.at[pl.ds(r * C, C)], in_sem.at[r]) for r in range(R)]
    for r in (1, 4, 2, 3, 0, 5):
        loads[r].start()
    load_species = pltpu.make_async_copy(species_in, species, in_sem.at[R])
    load_growth = pltpu.make_async_copy(growth_in, growth, in_sem.at[R + 1])
    load_prec = pltpu.make_async_copy(prec_in, prec, in_sem.at[R + 2])
    load_species.start()
    load_growth.start()
    load_prec.start()

    tmp[...] = jnp.zeros_like(tmp)
    tmp[0:R, :] = kap[...]
    kap_cols = tmp[...].T
    for r in range(R):
        kap_b[r + 1] = jnp.broadcast_to(kap_cols[:, r : r + 1], (C, T)) + 4.0

    pl.semaphore_wait(barrier, len(peers) + moved.astype(jnp.int32) + is_inner.astype(jnp.int32))

    def far_row(i):
        return remote(
            far_out.at[i], far_in.at[i], halo_s.at[4 + i], halo_r.at[4 + i], dev(up if i == 0 else dn, me)
        )

    halos = [
        remote(eff_in.at[pl.ds(0, C)], near.at[1], halo_s.at[0], halo_r.at[0], dev(up, me)),
        remote(eff_in.at[pl.ds(5 * C, C)], near.at[0], halo_s.at[1], halo_r.at[1], dev(dn, me)),
        remote(kap, kap_dn, halo_s.at[2], halo_r.at[2], dev(up, me)),
        remote(kap, kap_up, halo_s.at[3], halo_r.at[3], dev(dn, me)),
        far_row(0),
        far_row(1),
    ]
    for copy in halos[:4]:
        copy.start()
    for i, r in enumerate((1, 4)):
        loads[r].wait()
        far_out[i] = eff[r * C : (r + 1) * C, :].astype(BF)
        halos[4 + i].start()

    for r in (2, 3, 0, 5):
        loads[r].wait()

    def erow(r):
        if 0 <= r < R:
            return eff.at[pl.ds(r * C, C)]
        return {-2: far_in.at[1], -1: near.at[0], 6: near.at[1], 7: far_in.at[0]}[r]

    edge = lax.broadcasted_iota(jnp.int32, (C, T), 0)

    def stencil(centre, above, below, kappa):
        left = jnp.where(edge == 0, 0.0, pltpu.roll(centre, 1, 0))
        right = jnp.where(edge == C - 1, 0.0, pltpu.roll(centre, C - 1, 0))
        return kappa * centre - (below + above + right + left)

    def first_row(r):
        def body(c, carry):
            cs = pl.ds(pl.multiple_of(c * T, T), T)
            first[r + 1, :, cs] = stencil(
                erow(r)[:, cs], erow(r - 1)[:, cs].astype(F32), erow(r + 1)[:, cs].astype(F32), kap_b[r + 1]
            )
            return carry

        lax.fori_loop(0, W // T, body, 0)

    def spat_row(r):
        def body(c, carry):
            cs = pl.ds(pl.multiple_of(c * T, T), T)
            s = stencil(first[r + 1, :, cs], first[r, :, cs], first[r + 2, :, cs], kap_b[r + 1])
            spat[0, r * C : (r + 1) * C, cs] = s.astype(BF)
            return carry

        lax.fori_loop(0, W // T, body, 0)

    def piece(k, i):
        return spat.at[k, pl.ds(*CHUNKS[i])]

    def to_sib(i):
        return remote(piece(0, i), piece(1, i), ex_s.at[0, i], ex_r.at[0, i], dev(sp, sib))

    def to_far(i):
        return remote(piece(0, i), piece(2, i), ex_s.at[1, i], ex_r.at[1, i], dev(sp, far))

    def on(i):
        return remote(piece(2, i), piece(3, i), ex_s.at[2, i], ex_r.at[2, i], dev(sp, sib))

    def relay(j):
        return relayed.at[pl.ds(CHUNKS[j][0] - 2 * C, CHUNKS[j][1])]

    def to_relay(i, j):
        return remote(piece(0, j), relay(j), ex_s.at[1, j], relay_r.at[j], dev((dn, up)[i], me))

    def from_relay(i, j):
        return remote(relay(j), piece(2, j), relay_s.at[j], ex_r.at[1, j], dev((up, dn)[i], far))

    def pass_on(j):
        for i in range(2):

            @pl.when(inner[i])
            def _():
                to_relay(i, j).wait_recv()
                from_relay(i, j).start()

    def send(*chunks):
        for i in chunks:
            if i < 2:
                for t in range(2):

                    @pl.when(outer[t])
                    def _():
                        to_relay(t, i).start()

                @pl.when(is_inner)
                def _():
                    to_far(i).start()

            else:
                to_far(i).start()
            to_sib(i).start()

    lane = lax.broadcasted_iota(jnp.int32, (8, T), 1)
    low_iota = lax.broadcasted_iota(jnp.int32, (T, T), 0)
    sub = lax.broadcasted_iota(jnp.int32, (8, T), 0)
    nothing = jnp.zeros((8, T), F32)

    def trees(row_lo, row_hi):
        def step(g, r):
            start = r * C + g * GROUP
            for q in range(GROUP // 8):
                rows = pl.ds(pl.multiple_of(start + q * 8, 8), 8)
                ids = species[rows, :]
                live = lane < cnt_b[rows, :]
                high = jnp.where(live, lax.shift_right_arithmetic(ids, 7) - 4 * me, -1)
                low = ids & 127
                value = growth[rows, :].astype(BF).astype(F32)

                def left_side(p):
                    chosen = jnp.broadcast_to(high[p : p + 1, :], (8, T)) == (sub & 3)
                    held_value = jnp.where(sub < 4, jnp.broadcast_to(value[p : p + 1, :], (8, T)), 1.0)
                    return jnp.where(chosen, held_value, 0.0)

                def right_side(p):
                    same = jnp.broadcast_to(low[p : p + 1, :], (T, T)) == low_iota
                    return jnp.where(same, 1.0, 0.0).astype(BF)

                for p in range(0, 8, 2):
                    a = jnp.concatenate(
                        [
                            jnp.concatenate([left_side(p), nothing], 1),
                            jnp.concatenate([nothing, left_side(p + 1)], 1),
                        ],
                        0,
                    ).astype(BF)
                    b = jnp.concatenate([right_side(p), right_side(p + 1)], 1)
                    both = lax.dot_general(a, b, (((1,), (1,)), ((), ())), preferred_element_type=F32)
                    for j in range(2):
                        sums[pl.ds(g * GROUP + q * 8 + p + j, 8, stride=C), :] = both[j * 8 : (j + 1) * 8, :]
            return r

        def whole(r, carry):
            lax.fori_loop(0, C // GROUP, step, r)
            rows = pl.ds(pl.multiple_of(r * C, C), C)
            for h in range(4):
                cs = slice(h * T, (h + 1) * T)
                total = sums[h * C : (h + 1) * C, :]
                tally = sums[(h + 4) * C : (h + 5) * C, :]
                out[rows, cs] = noise[:, cs] * (total - tally * eff[rows, cs])
            return carry

        lax.fori_loop(row_lo, row_hi, whole, 0)

    def prior(ks, start, size, steps):
        def body(i, carry):
            rows = pl.ds(pl.multiple_of(start + i * size, 256), size)
            total = None
            for k in ks:
                q = prec[pl.ds(pl.multiple_of(block(k) * W, W), W), :]
                term = jnp.dot(spat[k, rows, :], q, preferred_element_type=F32)
                total = term if total is None else total + term
            out[rows, :] = out[rows, :] - total
            return carry

        lax.fori_loop(0, steps, body, 0)

    def store(i, start, size):
        rows = pl.ds(start, size)
        return pltpu.make_async_copy(out.at[rows], out_hbm.at[rows], out_sem.at[i])

    def gram_block(k):
        def body(i, carry):
            cs = pl.ds(pl.multiple_of(i * 256, 256), 256)
            part[k, :, cs] = jnp.dot(eff_t[...], spat[k, :, cs], preferred_element_type=F32).astype(BF)
            return carry

        lax.fori_loop(0, W // 256, body, 0)

    def gram_rows(k, starts, size, cs):
        total = None
        for r in starts:
            rows = slice(r * C, (r + size) * C)
            term = jnp.dot(eff_t[:, rows], spat[k, rows, cs], preferred_element_type=F32)
            total = term if total is None else total + term
        return total

    def gram_early(k):
        def body(i, carry):
            cs = pl.ds(pl.multiple_of(i * 256, 256), 256)
            late[k - 2, :, cs] = gram_rows(k, (1,), 1, cs) + gram_rows(k, (3,), 2, cs)
            return carry

        lax.fori_loop(0, W // 256, body, 0)

    def gram_late(k):
        def body(i, carry):
            cs = pl.ds(pl.multiple_of(i * 256, 256), 256)
            total = late[k - 2, :, cs] + gram_rows(k, (0, 2, 5), 1, cs)
            part[k, :, cs] = total.astype(BF)
            return carry

        lax.fori_loop(0, W // 256, body, 0)

    def z_peer(d):
        return dev(at(y, xh, (z + d) % 4), me)

    def gz(k, d):
        src = part.at[k, pl.ds(pl.multiple_of(((z + d) % 4) * 64, 64), 64)]
        return remote(src, rz.at[d - 1, k], gz_s.at[k, d - 1], gz_r.at[k, d - 1], z_peer(d))

    def y_peer(d):
        return dev(at((y + d) % 4, xh, z), me)

    def gy(k, d):
        src = part.at[k, pl.ds(256, 256), pl.ds(pl.multiple_of(((y + d) % 4) * T, T), T)]
        return remote(src, ry.at[d - 1, k], gy_s.at[k, d - 1], gy_r.at[k, d - 1], y_peer(d))

    def gram_send(k):
        for d in (1, 2, 3):
            gz(k, d).start()
            gy(k, d).start()

    def g2y(p, d):
        return remote(
            mid0.at[p, (y + d) % 4], ry2.at[p, d - 1], g2y_s.at[p, d - 1], g2y_r.at[p, d - 1], y_peer(d)
        )

    def g2z(p, d):
        src = mid1.at[p, pl.ds(pl.multiple_of(((z + d) % 4) * 64, 64), 64)]
        return remote(src, rz2.at[p, d - 1], g2z_s.at[p, d - 1], g2z_r.at[p, d - 1], z_peer(d))

    own_rows = pl.ds(pl.multiple_of(z * 64, 64), 64)
    own_cols = pl.ds(pl.multiple_of(y * T, T), T)

    def first_sums(p):
        for k in (2 * p, 2 * p + 1):
            cs = slice((k % 2) * T, (k % 2 + 1) * T)
            for d in (1, 2, 3):
                gz(k, d).wait_recv()
            total = part[k, own_rows, :].astype(F32)
            for d in (1, 2, 3):
                total = total + rz[d - 1, k].astype(F32)
            for q in range(4):
                mid0[p, q, :, cs] = total[:, q * T : (q + 1) * T].astype(BF)
        for d in (1, 2, 3):
            g2y(p, d).start()
        for k in (2 * p, 2 * p + 1):
            cs = slice((k % 2) * T, (k % 2 + 1) * T)
            for d in (1, 2, 3):
                gy(k, d).wait_recv()
            total = part[k, 256:512, own_cols].astype(F32)
            for d in (1, 2, 3):
                total = total + ry[d - 1, k].astype(F32)
            mid1[p, :, cs] = total.astype(BF)
        for d in (1, 2, 3):
            g2z(p, d).start()

    def to_result(away, k):
        h = 1 - xh if away else xh
        return remote(
            held.at[h, :, pl.ds(k * T, T)],
            fin.at[xh, :, own_cols],
            last_s.at[away, k],
            last_r.at[xh, y],
            dev(at(me, h, z), block(k)),
        )

    def arrived(h, q):
        return remote(
            held.at[0, :, pl.ds(0, T)], fin.at[h, :, pl.ds(q * T, T)], last_s.at[0, 0], last_r.at[h, q], dev(sp, sib)
        )

    def second_sums(p):
        cs = slice(p * 2 * T, (p + 1) * 2 * T)
        for d in (1, 2, 3):
            g2y(p, d).wait_recv()
        total = mid0[p, y].astype(F32)
        for d in (1, 2, 3):
            total = total + ry2[p, d - 1].astype(F32)
        held[0, :, cs] = total
        for d in (1, 2, 3):
            g2z(p, d).wait_recv()
        total = mid1[p, own_rows, :].astype(F32)
        for d in (1, 2, 3):
            total = total + rz2[p, d - 1].astype(F32)
        held[1, :, cs] = total
        for k in (2 * p, 2 * p + 1):
            to_result(1, k).start()
            if k:
                to_result(0, k).start()
            else:

                @pl.when(moved)
                def _():
                    to_result(0, 0).start()

                @pl.when(jnp.logical_not(moved))
                def _():
                    fin[xh, :, own_cols] = held[xh, :, 0:T]

    for r in (1, 2, 3, 4):
        first_row(r)
    spat_row(2)
    spat_row(3)
    send(2, 0, 1)
    tmp[0:R, :] = counts[...].astype(F32)
    cnt_cols = tmp[...].T
    for r in range(R):
        cnt_b[r * C : (r + 1) * C, :] = jnp.broadcast_to(cnt_cols[:, r : r + 1], (C, T)).astype(jnp.int32)
    load_species.wait()
    load_growth.wait()
    trees(0, 2)

    for i in range(4):
        halos[i].wait_recv()
    tmp[0:1, :] = kap_up[R - 1 : R, :]
    tmp[1:2, :] = kap_dn[0:1, :]
    kap_edge = tmp[...].T
    kap_b[0] = jnp.broadcast_to(kap_edge[:, 0:1], (C, T)) + 4.0
    kap_b[R + 1] = jnp.broadcast_to(kap_edge[:, 1:2], (C, T)) + 4.0

    @pl.when(sp == 0)
    def _():
        near[0] = jnp.zeros((C, W), F32)

    @pl.when(sp == 31)
    def _():
        near[1] = jnp.zeros((C, W), F32)

    first_row(0)
    first_row(5)
    spat_row(1)
    spat_row(4)
    send(3, 4)
    trees(2, 3)
    pass_on(0)
    pass_on(1)
    trees(3, 4)

    halos[4].wait_recv()
    halos[5].wait_recv()
    first_row(-1)
    first_row(6)

    @pl.when(sp == 0)
    def _():
        first[0] = jnp.zeros((C, W), F32)

    @pl.when(sp == 31)
    def _():
        first[R + 1] = jnp.zeros((C, W), F32)

    spat_row(0)
    spat_row(5)
    send(5, 6)

    for r in range(R):
        eff_t[:, r * C : (r + 1) * C] = eff[r * C : (r + 1) * C, :].T.astype(BF)
    gram_block(0)
    gram_send(0)
    for i in range(NC):
        to_sib(i).wait_recv()
    gram_block(1)
    gram_send(1)
    trees(4, 6)
    load_prec.wait()
    prior((0, 1), 0, 512, 3)

    for i in (2, 3, 4):
        to_far(i).wait_recv()
        on(i).start()
    first_sums(0)
    gram_early(2)
    for i in (2, 3, 4):
        on(i).wait_recv()
    gram_early(3)
    prior((2, 3), C, C, 1)
    prior((2, 3), 4 * C, C, 1)
    store(0, C, C).start()
    store(1, 4 * C, C).start()
    second_sums(0)

    for i in (5, 6, 0, 1):
        to_far(i).wait_recv()
        on(i).start()
    gram_late(2)
    gram_send(2)
    for i in (5, 6, 0, 1):
        on(i).wait_recv()
    gram_late(3)
    gram_send(3)
    prior((2, 3), 2 * C, 2 * C, 1)
    prior((2, 3), 0, C, 1)
    prior((2, 3), 5 * C, C, 1)
    store(2, 2 * C, 2 * C).start()
    store(3, 0, C).start()
    store(4, 5 * C, C).start()

    first_sums(1)
    second_sums(1)
    for h in range(2):
        for q in range(4):

            @pl.when(jnp.logical_or(jnp.logical_or(h != xh, q != y), moved))
            def _():
                arrived(h, q).wait_recv()

    gram[...] = (fin[0] + fin[1]) * (-0.5 / (NP * 32))

    for copy in halos:
        copy.wait_send()
    for i in range(NC):
        to_sib(i).wait_send()
        to_far(i).wait_send()
        on(i).wait_send()
    for j in range(2):

        @pl.when(is_inner)
        def _():
            from_relay(0, j).wait_send()

    for d in (1, 2, 3):
        for k in range(4):
            gz(k, d).wait_send()
            gy(k, d).wait_send()
        for p in range(2):
            g2y(p, d).wait_send()
            g2z(p, d).wait_send()
    for k in (1, 2, 3):
        to_result(1, k).wait_send()
        to_result(0, k).wait_send()
    to_result(1, 0).wait_send()

    @pl.when(moved)
    def _():
        to_result(0, 0).wait_send()

    for i, (start, size) in enumerate(((C, C), (4 * C, C), (2 * C, 2 * C), (0, C), (5 * C, C))):
        store(i, start, size).wait()


def finish(grad_in, gram_in, grad_out, gram_out, grad, gram, sem_in, sem_out):
    grad_rows = [pl.ds(r * C, C) for r in range(R)]
    loads = [pltpu.make_async_copy(grad_in.at[rows], grad.at[rows], sem_in.at[r]) for r, rows in enumerate(grad_rows)]
    loads.append(pltpu.make_async_copy(gram_in, gram, sem_in.at[R]))
    stores = [pltpu.make_async_copy(grad.at[rows], grad_out.at[rows], sem_out.at[r]) for r, rows in enumerate(grad_rows)]
    stores.append(pltpu.make_async_copy(gram, gram_out, sem_out.at[R]))
    for load in loads:
        load.start()
    for load, store in zip(loads, stores):
        load.wait()
        store.start()
    for store in stores:
        store.wait()


def shards(effects, kappa_sq, growth, tree_species, tree_counts, noise_precision, species_precision):
    vmem = pl.BlockSpec(memory_space=pltpu.VMEM)
    hbm = pl.BlockSpec(memory_space=pl.ANY)
    dma = pltpu.SemaphoreType.DMA
    grad, gram = pl.pallas_call(
        kernel,
        out_shape=(jax.ShapeDtypeStruct((NP, W), F32), jax.ShapeDtypeStruct((64, W), F32)),
        in_specs=[hbm, vmem, hbm, hbm, vmem, vmem, hbm],
        out_specs=(hbm, vmem),
        scratch_shapes=[
            pltpu.VMEM((NP, W), F32),
            pltpu.VMEM((NP, T), F32),
            pltpu.VMEM((NP, T), jnp.int32),
            pltpu.VMEM((4 * W, W), BF),
            pltpu.VMEM((NP, W), F32),
            pltpu.VMEM((2, C, W), F32),
            pltpu.VMEM((2, C, W), BF),
            pltpu.VMEM((2, C, W), BF),
            pltpu.VMEM((3 * C // 2, W), BF),
            pltpu.VMEM((R, C), F32),
            pltpu.VMEM((R, C), F32),
            pltpu.VMEM((8, C), F32),
            pltpu.VMEM((R + 2, C, T), F32),
            pltpu.VMEM((NP, T), jnp.int32),
            pltpu.VMEM((R + 2, C, W), F32),
            pltpu.VMEM((4, NP, W), BF),
            pltpu.VMEM((W, NP), BF),
            pltpu.VMEM((8 * C, T), F32),
            pltpu.VMEM((4, W, W), BF),
            pltpu.VMEM((2, W, W), F32),
            pltpu.VMEM((3, 4, 64, W), BF),
            pltpu.VMEM((3, 4, 256, T), BF),
            pltpu.VMEM((2, 4, 64, 2 * T), BF),
            pltpu.VMEM((2, 256, 2 * T), BF),
            pltpu.VMEM((2, 3, 64, 2 * T), BF),
            pltpu.VMEM((2, 3, 64, 2 * T), BF),
            pltpu.VMEM((2, 64, W), F32),
            pltpu.VMEM((2, 64, W), F32),
            dma((6,)), dma((6,)),
            dma((2,)), dma((2,)),
            dma((3, NC)), dma((3, NC)),
            dma((4, 3)), dma((4, 3)),
            dma((4, 3)), dma((4, 3)),
            dma((2, 3)), dma((2, 3)),
            dma((2, 3)), dma((2, 3)),
            dma((2, 4)), dma((2, 4)),
            dma((R + 3,)),
            dma((5,)),
        ],
        compiler_params=pltpu.CompilerParams(
            collective_id=0, has_side_effects=True, vmem_limit_bytes=56 << 20
        ),
        cost_estimate=pl.CostEstimate(flops=7_000_000_000, bytes_accessed=12_000_000, transcendentals=0),
        name="posterior_gradient",
    )(
        effects.reshape(NP, W),
        kappa_sq,
        growth.reshape(NP, T),
        tree_species.reshape(NP, T),
        tree_counts,
        noise_precision.reshape(1, W),
        species_precision,
    )
    grad, gram = pl.pallas_call(
        finish,
        out_shape=(jax.ShapeDtypeStruct((NP, W), F32), jax.ShapeDtypeStruct((64, W), F32)),
        in_specs=[hbm, hbm],
        out_specs=(hbm, hbm),
        scratch_shapes=[pltpu.VMEM((NP, W), F32), pltpu.VMEM((64, W), F32), dma((R + 1,)), dma((R + 1,))],
        compiler_params=pltpu.CompilerParams(vmem_limit_bytes=56 << 20),
        name="finish",
    )(grad, gram)
    return grad.reshape(R, C, W), gram


def solution(mesh):
    return jax.shard_map(
        shards,
        mesh=mesh,
        in_specs=(
            P("space", None, "species"),
            P("space", None),
            P("space", None, None),
            P("space", None, None),
            P("space", None),
            P("species"),
            P(None, "species"),
        ),
        out_specs=(P("space", None, "species"), P("space", "species")),
        check_vma=False,
    )
```

```python
import jax
import jax.numpy as jnp
from jax import lax
from jax.experimental import pallas as pl
from jax.experimental.pallas import tpu as pltpu
from jax.sharding import PartitionSpec as P

MESH = pl.DeviceIdType.MESH
BF = jnp.bfloat16
F32 = jnp.float32
R, C, W, T = 6, 256, 512, 128
NP = R * C
GROUP = 32
CHUNKS = ((2 * C, C // 2), (2 * C + C // 2, C // 2), (3 * C, C), (C, C), (4 * C, C), (0, C), (5 * C, C))
NC = len(CHUNKS)


def kernel(
    eff_in, kap, growth_in, species_in, counts, noise, prec_in,
    out_hbm, gram,
    eff, growth, species, prec, out,
    near, far_out, far_in, relayed, kap_up, kap_dn, tmp, kap_b, cnt_b, first, spat, eff_t, sums,
    part, late, rz, ry, mid0, mid1, rz2, ry2, held, fin,
    halo_s, halo_r, relay_s, relay_r, ex_s, ex_r, gz_s, gz_r, gy_s, gy_r, g2y_s, g2y_r, g2z_s, g2z_r, last_s, last_r, in_sem, out_sem,
):
    sp, me = lax.axis_index("space"), lax.axis_index("species")
    z, xh, y = sp % 4, (sp // 4) % 2, sp // 8
    up, dn = (sp + 31) % 32, (sp + 1) % 32
    sib = (me // 2) * 2 + (me + 1) % 2
    far = (me + 2) % 4

    def at(yy, hh, zz):
        return (yy * 2 + hh) * 4 + zz

    def dev(space, spec):
        return {"space": space, "species": spec}

    def block(k):
        return ((me // 2 + k // 2) % 2) * 2 + (me % 2 + k % 2) % 2

    moved = y != me

    def remote(src, dst, ssem, rsem, to):
        return pltpu.make_async_remote_copy(
            src_ref=src, dst_ref=dst, send_sem=ssem, recv_sem=rsem, device_id=to, device_id_type=MESH
        )

    loads = [pltpu.make_async_copy(eff_in.at[pl.ds(r * C, C)], eff.at[pl.ds(r * C, C)], in_sem.at[r]) for r in range(R)]
    for r in (1, 4, 2, 3, 0, 5):
        loads[r].start()
    load_species = pltpu.make_async_copy(species_in, species, in_sem.at[R])
    load_growth = pltpu.make_async_copy(growth_in, growth, in_sem.at[R + 1])
    load_prec = pltpu.make_async_copy(prec_in, prec, in_sem.at[R + 2])
    load_species.start()
    load_growth.start()
    load_prec.start()

    barrier = pltpu.get_barrier_semaphore()
    peers = [dev(up, me), dev(dn, me), dev(sp, sib), dev(sp, far)]
    peers += [dev(at(y, xh, (z + d) % 4), me) for d in (1, 2, 3)]
    peers += [dev(at((y + d) % 4, xh, z), me) for d in (1, 2, 3)]
    peers += [dev(at((y + d) % 4, h, z), y) for d in (1, 2, 3) for h in (0, 1)]
    peers += [dev(at(y, 1 - xh, z), y)]
    for peer in peers:
        pl.semaphore_signal(barrier, inc=1, device_id=peer, device_id_type=MESH)

    @pl.when(moved)
    def _():
        pl.semaphore_signal(barrier, inc=1, device_id=dev(sp, y), device_id_type=MESH)

    outer = (z == 0, z == 3)
    inner = (z == 1, z == 2)
    for i in range(2):

        @pl.when(outer[i])
        def _():
            pl.semaphore_signal(barrier, inc=1, device_id=dev((dn, up)[i], far), device_id_type=MESH)

    is_inner = jnp.logical_or(z == 1, z == 2)

    tmp[...] = jnp.zeros_like(tmp)
    tmp[0:R, :] = kap[...]
    kap_cols = tmp[...].T
    for r in range(R):
        kap_b[r + 1] = jnp.broadcast_to(kap_cols[:, r : r + 1], (C, T)) + 4.0

    pl.semaphore_wait(barrier, len(peers) + moved.astype(jnp.int32) + is_inner.astype(jnp.int32))

    def far_row(i):
        return remote(
            far_out.at[i], far_in.at[i], halo_s.at[4 + i], halo_r.at[4 + i], dev(up if i == 0 else dn, me)
        )

    halos = [
        remote(eff_in.at[pl.ds(0, C)], near.at[1], halo_s.at[0], halo_r.at[0], dev(up, me)),
        remote(eff_in.at[pl.ds(5 * C, C)], near.at[0], halo_s.at[1], halo_r.at[1], dev(dn, me)),
        remote(kap, kap_dn, halo_s.at[2], halo_r.at[2], dev(up, me)),
        remote(kap, kap_up, halo_s.at[3], halo_r.at[3], dev(dn, me)),
        far_row(0),
        far_row(1),
    ]
    for copy in halos[:4]:
        copy.start()
    for i, r in enumerate((1, 4)):
        loads[r].wait()
        far_out[i] = eff[r * C : (r + 1) * C, :].astype(BF)
        halos[4 + i].start()

    for r in (2, 3, 0, 5):
        loads[r].wait()

    def erow(r):
        if 0 <= r < R:
            return eff.at[pl.ds(r * C, C)]
        return {-2: far_in.at[1], -1: near.at[0], 6: near.at[1], 7: far_in.at[0]}[r]

    edge = lax.broadcasted_iota(jnp.int32, (C, T), 0)

    def stencil(centre, above, below, kappa):
        left = jnp.where(edge == 0, 0.0, pltpu.roll(centre, 1, 0))
        right = jnp.where(edge == C - 1, 0.0, pltpu.roll(centre, C - 1, 0))
        return kappa * centre - (below + above + right + left)

    def first_row(r):
        def body(c, carry):
            cs = pl.ds(pl.multiple_of(c * T, T), T)
            first[r + 1, :, cs] = stencil(
                erow(r)[:, cs], erow(r - 1)[:, cs].astype(F32), erow(r + 1)[:, cs].astype(F32), kap_b[r + 1]
            )
            return carry

        lax.fori_loop(0, W // T, body, 0)

    def spat_row(r):
        def body(c, carry):
            cs = pl.ds(pl.multiple_of(c * T, T), T)
            s = stencil(first[r + 1, :, cs], first[r, :, cs], first[r + 2, :, cs], kap_b[r + 1])
            spat[0, r * C : (r + 1) * C, cs] = s.astype(BF)
            return carry

        lax.fori_loop(0, W // T, body, 0)

    def piece(k, i):
        return spat.at[k, pl.ds(*CHUNKS[i])]

    def to_sib(i):
        return remote(piece(0, i), piece(1, i), ex_s.at[0, i], ex_r.at[0, i], dev(sp, sib))

    def to_far(i):
        return remote(piece(0, i), piece(2, i), ex_s.at[1, i], ex_r.at[1, i], dev(sp, far))

    def on(i):
        return remote(piece(2, i), piece(3, i), ex_s.at[2, i], ex_r.at[2, i], dev(sp, sib))

    def relay(j):
        return relayed.at[pl.ds(CHUNKS[j][0] - 2 * C, CHUNKS[j][1])]

    def to_relay(i, j):
        return remote(piece(0, j), relay(j), ex_s.at[1, j], relay_r.at[j], dev((dn, up)[i], me))

    def from_relay(i, j):
        return remote(relay(j), piece(2, j), relay_s.at[j], ex_r.at[1, j], dev((up, dn)[i], far))

    def pass_on(j):
        for i in range(2):

            @pl.when(inner[i])
            def _():
                to_relay(i, j).wait_recv()
                from_relay(i, j).start()

    def send(*chunks):
        for i in chunks:
            if i < 2:
                for t in range(2):

                    @pl.when(outer[t])
                    def _():
                        to_relay(t, i).start()

                @pl.when(is_inner)
                def _():
                    to_far(i).start()

            else:
                to_far(i).start()
            to_sib(i).start()

    lane = lax.broadcasted_iota(jnp.int32, (8, T), 1)
    low_iota = lax.broadcasted_iota(jnp.int32, (T, T), 0)
    sub = lax.broadcasted_iota(jnp.int32, (8, T), 0)
    nothing = jnp.zeros((8, T), F32)

    def trees(row_lo, row_hi):
        def step(g, r):
            start = r * C + g * GROUP
            for q in range(GROUP // 8):
                rows = pl.ds(pl.multiple_of(start + q * 8, 8), 8)
                ids = species[rows, :]
                live = lane < cnt_b[rows, :]
                high = jnp.where(live, lax.shift_right_arithmetic(ids, 7) - 4 * me, -1)
                low = ids & 127
                value = growth[rows, :].astype(BF).astype(F32)

                def left_side(p):
                    chosen = jnp.broadcast_to(high[p : p + 1, :], (8, T)) == (sub & 3)
                    held_value = jnp.where(sub < 4, jnp.broadcast_to(value[p : p + 1, :], (8, T)), 1.0)
                    return jnp.where(chosen, held_value, 0.0)

                def right_side(p):
                    same = jnp.broadcast_to(low[p : p + 1, :], (T, T)) == low_iota
                    return jnp.where(same, 1.0, 0.0).astype(BF)

                for p in range(0, 8, 2):
                    a = jnp.concatenate(
                        [
                            jnp.concatenate([left_side(p), nothing], 1),
                            jnp.concatenate([nothing, left_side(p + 1)], 1),
                        ],
                        0,
                    ).astype(BF)
                    b = jnp.concatenate([right_side(p), right_side(p + 1)], 1)
                    both = lax.dot_general(a, b, (((1,), (1,)), ((), ())), preferred_element_type=F32)
                    for j in range(2):
                        sums[pl.ds(g * GROUP + q * 8 + p + j, 8, stride=C), :] = both[j * 8 : (j + 1) * 8, :]
            return r

        def whole(r, carry):
            lax.fori_loop(0, C // GROUP, step, r)
            rows = pl.ds(pl.multiple_of(r * C, C), C)
            for h in range(4):
                cs = slice(h * T, (h + 1) * T)
                total = sums[h * C : (h + 1) * C, :]
                tally = sums[(h + 4) * C : (h + 5) * C, :]
                out[rows, cs] = noise[:, cs] * (total - tally * eff[rows, cs])
            return carry

        lax.fori_loop(row_lo, row_hi, whole, 0)

    def prior(ks, start, size, steps):
        def body(i, carry):
            rows = pl.ds(pl.multiple_of(start + i * size, 256), size)
            total = None
            for k in ks:
                q = prec[pl.ds(pl.multiple_of(block(k) * W, W), W), :]
                term = jnp.dot(spat[k, rows, :], q, preferred_element_type=F32)
                total = term if total is None else total + term
            out[rows, :] = out[rows, :] - total
            return carry

        lax.fori_loop(0, steps, body, 0)

    def store(i, start, size):
        rows = pl.ds(start, size)
        return pltpu.make_async_copy(out.at[rows], out_hbm.at[rows], out_sem.at[i])

    def gram_block(k):
        def body(i, carry):
            cs = pl.ds(pl.multiple_of(i * 256, 256), 256)
            part[k, :, cs] = jnp.dot(eff_t[...], spat[k, :, cs], preferred_element_type=F32).astype(BF)
            return carry

        lax.fori_loop(0, W // 256, body, 0)

    def gram_rows(k, starts, size, cs):
        total = None
        for r in starts:
            rows = slice(r * C, (r + size) * C)
            term = jnp.dot(eff_t[:, rows], spat[k, rows, cs], preferred_element_type=F32)
            total = term if total is None else total + term
        return total

    def gram_early(k):
        def body(i, carry):
            cs = pl.ds(pl.multiple_of(i * 256, 256), 256)
            late[k - 2, :, cs] = gram_rows(k, (1,), 1, cs) + gram_rows(k, (3,), 2, cs)
            return carry

        lax.fori_loop(0, W // 256, body, 0)

    def gram_late(k):
        def body(i, carry):
            cs = pl.ds(pl.multiple_of(i * 256, 256), 256)
            total = late[k - 2, :, cs] + gram_rows(k, (0, 2, 5), 1, cs)
            part[k, :, cs] = total.astype(BF)
            return carry

        lax.fori_loop(0, W // 256, body, 0)

    def z_peer(d):
        return dev(at(y, xh, (z + d) % 4), me)

    def gz(k, d):
        src = part.at[k, pl.ds(pl.multiple_of(((z + d) % 4) * 64, 64), 64)]
        return remote(src, rz.at[d - 1, k], gz_s.at[k, d - 1], gz_r.at[k, d - 1], z_peer(d))

    def y_peer(d):
        return dev(at((y + d) % 4, xh, z), me)

    def gy(k, d):
        src = part.at[k, pl.ds(256, 256), pl.ds(pl.multiple_of(((y + d) % 4) * T, T), T)]
        return remote(src, ry.at[d - 1, k], gy_s.at[k, d - 1], gy_r.at[k, d - 1], y_peer(d))

    def gram_send(k):
        for d in (1, 2, 3):
            gz(k, d).start()
            gy(k, d).start()

    def g2y(p, d):
        return remote(
            mid0.at[p, (y + d) % 4], ry2.at[p, d - 1], g2y_s.at[p, d - 1], g2y_r.at[p, d - 1], y_peer(d)
        )

    def g2z(p, d):
        src = mid1.at[p, pl.ds(pl.multiple_of(((z + d) % 4) * 64, 64), 64)]
        return remote(src, rz2.at[p, d - 1], g2z_s.at[p, d - 1], g2z_r.at[p, d - 1], z_peer(d))

    own_rows = pl.ds(pl.multiple_of(z * 64, 64), 64)
    own_cols = pl.ds(pl.multiple_of(y * T, T), T)

    def first_sums(p):
        for k in (2 * p, 2 * p + 1):
            cs = slice((k % 2) * T, (k % 2 + 1) * T)
            for d in (1, 2, 3):
                gz(k, d).wait_recv()
            total = part[k, own_rows, :].astype(F32)
            for d in (1, 2, 3):
                total = total + rz[d - 1, k].astype(F32)
            for q in range(4):
                mid0[p, q, :, cs] = total[:, q * T : (q + 1) * T].astype(BF)
        for d in (1, 2, 3):
            g2y(p, d).start()
        for k in (2 * p, 2 * p + 1):
            cs = slice((k % 2) * T, (k % 2 + 1) * T)
            for d in (1, 2, 3):
                gy(k, d).wait_recv()
            total = part[k, 256:512, own_cols].astype(F32)
            for d in (1, 2, 3):
                total = total + ry[d - 1, k].astype(F32)
            mid1[p, :, cs] = total.astype(BF)
        for d in (1, 2, 3):
            g2z(p, d).start()

    def to_result(h, k):
        return remote(
            held.at[h, :, pl.ds(k * T, T)],
            fin.at[xh, :, own_cols],
            last_s.at[h, k],
            last_r.at[xh, y],
            dev(at(me, h, z), block(k)),
        )

    def leaves(h):
        return jnp.logical_or(h != xh, moved)

    def results(p, h):
        for k in (2 * p, 2 * p + 1):
            if k:
                to_result(h, k).start()
            else:

                @pl.when(leaves(h))
                def _():
                    to_result(h, 0).start()

                @pl.when(jnp.logical_not(leaves(h)))
                def _():
                    fin[xh, :, own_cols] = held[h, :, 0:T]

    def arrived(h, q):
        return remote(
            held.at[0, :, pl.ds(0, T)], fin.at[h, :, pl.ds(q * T, T)], last_s.at[0, 0], last_r.at[h, q], dev(sp, sib)
        )

    def second_sums(p):
        cs = slice(p * 2 * T, (p + 1) * 2 * T)
        for d in (1, 2, 3):
            g2y(p, d).wait_recv()
        total = mid0[p, y].astype(F32)
        for d in (1, 2, 3):
            total = total + ry2[p, d - 1].astype(F32)
        held[0, :, cs] = total.astype(BF)
        results(p, 0)
        for d in (1, 2, 3):
            g2z(p, d).wait_recv()
        total = mid1[p, own_rows, :].astype(F32)
        for d in (1, 2, 3):
            total = total + rz2[p, d - 1].astype(F32)
        held[1, :, cs] = total.astype(BF)
        results(p, 1)

    for r in (1, 2, 3, 4):
        first_row(r)
    spat_row(2)
    spat_row(3)
    send(2, 0, 1)
    tmp[0:R, :] = counts[...].astype(F32)
    cnt_cols = tmp[...].T
    for r in range(R):
        cnt_b[r * C : (r + 1) * C, :] = jnp.broadcast_to(cnt_cols[:, r : r + 1], (C, T)).astype(jnp.int32)
    load_species.wait()
    load_growth.wait()
    trees(0, 2)

    for i in range(4):
        halos[i].wait_recv()
    tmp[0:1, :] = kap_up[R - 1 : R, :]
    tmp[1:2, :] = kap_dn[0:1, :]
    kap_edge = tmp[...].T
    kap_b[0] = jnp.broadcast_to(kap_edge[:, 0:1], (C, T)) + 4.0
    kap_b[R + 1] = jnp.broadcast_to(kap_edge[:, 1:2], (C, T)) + 4.0

    @pl.when(sp == 0)
    def _():
        near[0] = jnp.zeros((C, W), F32)

    @pl.when(sp == 31)
    def _():
        near[1] = jnp.zeros((C, W), F32)

    first_row(0)
    first_row(5)
    spat_row(1)
    spat_row(4)
    send(3, 4)
    trees(2, 3)
    pass_on(0)
    pass_on(1)
    trees(3, 4)

    halos[4].wait_recv()
    halos[5].wait_recv()
    first_row(-1)
    first_row(6)

    @pl.when(sp == 0)
    def _():
        first[0] = jnp.zeros((C, W), F32)

    @pl.when(sp == 31)
    def _():
        first[R + 1] = jnp.zeros((C, W), F32)

    spat_row(0)
    spat_row(5)
    send(5, 6)

    for r in range(R):
        eff_t[:, r * C : (r + 1) * C] = eff[r * C : (r + 1) * C, :].T.astype(BF)
    gram_block(0)
    gram_send(0)
    for i in range(NC):
        to_sib(i).wait_recv()
    gram_block(1)
    gram_send(1)
    trees(4, 6)
    load_prec.wait()
    prior((0, 1), 0, 512, 3)

    for i in (2, 3, 4):
        to_far(i).wait_recv()
        on(i).start()
    first_sums(0)
    gram_early(2)
    for i in (2, 3, 4):
        on(i).wait_recv()
    gram_early(3)
    prior((2, 3), C, C, 1)
    prior((2, 3), 4 * C, C, 1)
    store(0, C, C).start()
    store(1, 4 * C, C).start()
    second_sums(0)

    for i in (5, 6, 0, 1):
        to_far(i).wait_recv()
        on(i).start()
    gram_late(2)
    gram_send(2)
    for i in (5, 6, 0, 1):
        on(i).wait_recv()
    gram_late(3)
    gram_send(3)
    prior((2, 3), 2 * C, 2 * C, 1)
    prior((2, 3), 0, C, 1)
    prior((2, 3), 5 * C, C, 1)
    store(2, 2 * C, 2 * C).start()
    store(3, 0, C).start()
    store(4, 5 * C, C).start()

    first_sums(1)
    second_sums(1)
    for h in range(2):
        for q in range(4):

            @pl.when(jnp.logical_or(jnp.logical_or(h != xh, q != y), moved))
            def _():
                arrived(h, q).wait_recv()

    gram[...] = (fin[0].astype(F32) + fin[1].astype(F32)) * (-0.5 / (NP * 32))

    for copy in halos:
        copy.wait_send()
    for i in range(NC):
        to_sib(i).wait_send()
        to_far(i).wait_send()
        on(i).wait_send()
    for j in range(2):

        @pl.when(is_inner)
        def _():
            from_relay(0, j).wait_send()

    for d in (1, 2, 3):
        for k in range(4):
            gz(k, d).wait_send()
            gy(k, d).wait_send()
        for p in range(2):
            g2y(p, d).wait_send()
            g2z(p, d).wait_send()
    for h in range(2):
        for k in (1, 2, 3):
            to_result(h, k).wait_send()

        @pl.when(leaves(h))
        def _():
            to_result(h, 0).wait_send()

    for i, (start, size) in enumerate(((C, C), (4 * C, C), (2 * C, 2 * C), (0, C), (5 * C, C))):
        store(i, start, size).wait()


def finish(grad_in, gram_in, grad_out, gram_out, grad, gram, sem_in, sem_out):
    grad_rows = [pl.ds(r * C, C) for r in range(R)]
    loads = [pltpu.make_async_copy(grad_in.at[rows], grad.at[rows], sem_in.at[r]) for r, rows in enumerate(grad_rows)]
    loads.append(pltpu.make_async_copy(gram_in, gram, sem_in.at[R]))
    stores = [pltpu.make_async_copy(grad.at[rows], grad_out.at[rows], sem_out.at[r]) for r, rows in enumerate(grad_rows)]
    stores.append(pltpu.make_async_copy(gram, gram_out, sem_out.at[R]))
    for load in loads:
        load.start()
    for load, store in zip(loads, stores):
        load.wait()
        store.start()
    for store in stores:
        store.wait()


def shards(effects, kappa_sq, growth, tree_species, tree_counts, noise_precision, species_precision):
    vmem = pl.BlockSpec(memory_space=pltpu.VMEM)
    hbm = pl.BlockSpec(memory_space=pl.ANY)
    dma = pltpu.SemaphoreType.DMA
    grad, gram = pl.pallas_call(
        kernel,
        out_shape=(jax.ShapeDtypeStruct((NP, W), F32), jax.ShapeDtypeStruct((64, W), F32)),
        in_specs=[hbm, vmem, hbm, hbm, vmem, vmem, hbm],
        out_specs=(hbm, vmem),
        scratch_shapes=[
            pltpu.VMEM((NP, W), F32),
            pltpu.VMEM((NP, T), F32),
            pltpu.VMEM((NP, T), jnp.int32),
            pltpu.VMEM((4 * W, W), BF),
            pltpu.VMEM((NP, W), F32),
            pltpu.VMEM((2, C, W), F32),
            pltpu.VMEM((2, C, W), BF),
            pltpu.VMEM((2, C, W), BF),
            pltpu.VMEM((3 * C // 2, W), BF),
            pltpu.VMEM((R, C), F32),
            pltpu.VMEM((R, C), F32),
            pltpu.VMEM((8, C), F32),
            pltpu.VMEM((R + 2, C, T), F32),
            pltpu.VMEM((NP, T), jnp.int32),
            pltpu.VMEM((R + 2, C, W), F32),
            pltpu.VMEM((4, NP, W), BF),
            pltpu.VMEM((W, NP), BF),
            pltpu.VMEM((8 * C, T), F32),
            pltpu.VMEM((4, W, W), BF),
            pltpu.VMEM((2, W, W), F32),
            pltpu.VMEM((3, 4, 64, W), BF),
            pltpu.VMEM((3, 4, 256, T), BF),
            pltpu.VMEM((2, 4, 64, 2 * T), BF),
            pltpu.VMEM((2, 256, 2 * T), BF),
            pltpu.VMEM((2, 3, 64, 2 * T), BF),
            pltpu.VMEM((2, 3, 64, 2 * T), BF),
            pltpu.VMEM((2, 64, W), BF),
            pltpu.VMEM((2, 64, W), BF),
            dma((6,)), dma((6,)),
            dma((2,)), dma((2,)),
            dma((3, NC)), dma((3, NC)),
            dma((4, 3)), dma((4, 3)),
            dma((4, 3)), dma((4, 3)),
            dma((2, 3)), dma((2, 3)),
            dma((2, 3)), dma((2, 3)),
            dma((2, 4)), dma((2, 4)),
            dma((R + 3,)),
            dma((5,)),
        ],
        compiler_params=pltpu.CompilerParams(
            collective_id=0, has_side_effects=True, vmem_limit_bytes=56 << 20
        ),
        cost_estimate=pl.CostEstimate(flops=7_000_000_000, bytes_accessed=12_000_000, transcendentals=0),
        name="posterior_gradient",
    )(
        effects.reshape(NP, W),
        kappa_sq,
        growth.reshape(NP, T),
        tree_species.reshape(NP, T),
        tree_counts,
        noise_precision.reshape(1, W),
        species_precision,
    )
    grad, gram = pl.pallas_call(
        finish,
        out_shape=(jax.ShapeDtypeStruct((NP, W), F32), jax.ShapeDtypeStruct((64, W), F32)),
        in_specs=[hbm, hbm],
        out_specs=(hbm, hbm),
        scratch_shapes=[pltpu.VMEM((NP, W), F32), pltpu.VMEM((64, W), F32), dma((R + 1,)), dma((R + 1,))],
        compiler_params=pltpu.CompilerParams(vmem_limit_bytes=56 << 20),
        name="finish",
    )(grad, gram)
    return grad.reshape(R, C, W), gram


def solution(mesh):
    return jax.shard_map(
        shards,
        mesh=mesh,
        in_specs=(
            P("space", None, "species"),
            P("space", None),
            P("space", None, None),
            P("space", None, None),
            P("space", None),
            P("species"),
            P(None, "species"),
        ),
        out_specs=(P("space", None, "species"), P("space", "species")),
        check_vma=False,
    )
```

```python
import jax
import jax.numpy as jnp
from jax import lax
from jax.experimental import pallas as pl
from jax.experimental.pallas import tpu as pltpu
from jax.sharding import PartitionSpec as P

MESH = pl.DeviceIdType.MESH
BF = jnp.bfloat16
F32 = jnp.float32
R, C, W, T = 6, 256, 512, 128
NP = R * C
GROUP = 32
CHUNKS = ((2 * C, C // 2), (2 * C + C // 2, C // 2), (3 * C, C), (C, C), (4 * C, C), (0, C), (5 * C, C))
NC = len(CHUNKS)


def kernel(
    eff_in, kap, growth_in, species_in, counts, noise, prec_in,
    out_hbm, gram,
    eff, growth, species, prec, out,
    near, far_out, far_in, relayed, kap_up, kap_dn, tmp, kap_b, cnt_b, first, spat, eff_t, sums,
    part, late, rz, ry, mid0, mid1, rz2, ry2, held, fin,
    halo_s, halo_r, relay_s, relay_r, ex_s, ex_r, gz_s, gz_r, gy_s, gy_r, g2y_s, g2y_r, g2z_s, g2z_r, last_s, last_r, in_sem, out_sem,
):
    sp, me = lax.axis_index("space"), lax.axis_index("species")
    z, xh, y = sp % 4, (sp // 4) % 2, sp // 8
    up, dn = (sp + 31) % 32, (sp + 1) % 32
    sib = (me // 2) * 2 + (me + 1) % 2
    far = (me + 2) % 4

    def at(yy, hh, zz):
        return (yy * 2 + hh) * 4 + zz

    def dev(space, spec):
        return {"space": space, "species": spec}

    def block(k):
        return ((me // 2 + k // 2) % 2) * 2 + (me % 2 + k % 2) % 2

    moved = y != me

    def remote(src, dst, ssem, rsem, to):
        return pltpu.make_async_remote_copy(
            src_ref=src, dst_ref=dst, send_sem=ssem, recv_sem=rsem, device_id=to, device_id_type=MESH
        )

    loads = [pltpu.make_async_copy(eff_in.at[pl.ds(r * C, C)], eff.at[pl.ds(r * C, C)], in_sem.at[r]) for r in range(R)]
    for r in (1, 4, 2, 3, 0, 5):
        loads[r].start()
    load_species = pltpu.make_async_copy(species_in, species, in_sem.at[R])
    load_growth = pltpu.make_async_copy(growth_in, growth, in_sem.at[R + 1])
    load_prec = pltpu.make_async_copy(prec_in, prec, in_sem.at[R + 2])
    load_species.start()
    load_growth.start()
    load_prec.start()

    barrier = pltpu.get_barrier_semaphore()
    peers = [dev(up, me), dev(dn, me), dev(sp, sib), dev(sp, far)]
    peers += [dev(at(y, xh, (z + d) % 4), me) for d in (1, 2, 3)]
    peers += [dev(at((y + d) % 4, xh, z), me) for d in (1, 2, 3)]
    peers += [dev(at((y + d) % 4, h, z), y) for d in (1, 2, 3) for h in (0, 1)]
    peers += [dev(at(y, 1 - xh, z), y)]
    for peer in peers:
        pl.semaphore_signal(barrier, inc=1, device_id=peer, device_id_type=MESH)

    @pl.when(moved)
    def _():
        pl.semaphore_signal(barrier, inc=1, device_id=dev(sp, y), device_id_type=MESH)

    outer = (z == 0, z == 3)
    inner = (z == 1, z == 2)
    for i in range(2):

        @pl.when(outer[i])
        def _():
            pl.semaphore_signal(barrier, inc=1, device_id=dev((dn, up)[i], far), device_id_type=MESH)

    is_inner = jnp.logical_or(z == 1, z == 2)

    tmp[...] = jnp.zeros_like(tmp)
    tmp[0:R, :] = kap[...]
    kap_cols = tmp[...].T
    for r in range(R):
        kap_b[r + 1] = jnp.broadcast_to(kap_cols[:, r : r + 1], (C, T)) + 4.0

    pl.semaphore_wait(barrier, len(peers) + moved.astype(jnp.int32) + is_inner.astype(jnp.int32))

    def far_row(i):
        return remote(
            far_out.at[i], far_in.at[i], halo_s.at[4 + i], halo_r.at[4 + i], dev(up if i == 0 else dn, me)
        )

    halos = [
        remote(eff_in.at[pl.ds(0, C)], near.at[1], halo_s.at[0], halo_r.at[0], dev(up, me)),
        remote(eff_in.at[pl.ds(5 * C, C)], near.at[0], halo_s.at[1], halo_r.at[1], dev(dn, me)),
        remote(kap, kap_dn, halo_s.at[2], halo_r.at[2], dev(up, me)),
        remote(kap, kap_up, halo_s.at[3], halo_r.at[3], dev(dn, me)),
        far_row(0),
        far_row(1),
    ]
    for copy in halos[:4]:
        copy.start()
    for r in (1, 4, 2, 3, 0, 5):
        loads[r].wait()

    def erow(r):
        if 0 <= r < R:
            return eff.at[pl.ds(r * C, C)]
        return {-2: far_in.at[1], -1: near.at[0], 6: near.at[1], 7: far_in.at[0]}[r]

    edge = lax.broadcasted_iota(jnp.int32, (C, T), 0)

    def stencil(centre, above, below, kappa):
        left = jnp.where(edge == 0, 0.0, pltpu.roll(centre, 1, 0))
        right = jnp.where(edge == C - 1, 0.0, pltpu.roll(centre, C - 1, 0))
        return kappa * centre - (below + above + right + left)

    def first_row(r):
        def body(c, carry):
            cs = pl.ds(pl.multiple_of(c * T, T), T)
            first[r + 1, :, cs] = stencil(
                erow(r)[:, cs], erow(r - 1)[:, cs].astype(F32), erow(r + 1)[:, cs].astype(F32), kap_b[r + 1]
            )
            return carry

        lax.fori_loop(0, W // T, body, 0)

    def spat_row(r):
        def body(c, carry):
            cs = pl.ds(pl.multiple_of(c * T, T), T)
            s = stencil(first[r + 1, :, cs], first[r, :, cs], first[r + 2, :, cs], kap_b[r + 1])
            spat[0, r * C : (r + 1) * C, cs] = s.astype(BF)
            return carry

        lax.fori_loop(0, W // T, body, 0)

    def piece(k, i):
        return spat.at[k, pl.ds(*CHUNKS[i])]

    def to_sib(i):
        return remote(piece(0, i), piece(1, i), ex_s.at[0, i], ex_r.at[0, i], dev(sp, sib))

    def to_far(i):
        return remote(piece(0, i), piece(2, i), ex_s.at[1, i], ex_r.at[1, i], dev(sp, far))

    def on(i):
        return remote(piece(2, i), piece(3, i), ex_s.at[2, i], ex_r.at[2, i], dev(sp, sib))

    def relay(j):
        return relayed.at[pl.ds(CHUNKS[j][0] - 2 * C, CHUNKS[j][1])]

    def to_relay(i, j):
        return remote(piece(0, j), relay(j), ex_s.at[1, j], relay_r.at[j], dev((dn, up)[i], me))

    def from_relay(i, j):
        return remote(relay(j), piece(2, j), relay_s.at[j], ex_r.at[1, j], dev((up, dn)[i], far))

    def pass_on(j):
        for i in range(2):

            @pl.when(inner[i])
            def _():
                to_relay(i, j).wait_recv()
                from_relay(i, j).start()

    def send(*chunks):
        for i in chunks:
            if i < 2:
                for t in range(2):

                    @pl.when(outer[t])
                    def _():
                        to_relay(t, i).start()

                @pl.when(is_inner)
                def _():
                    to_far(i).start()

            else:
                to_far(i).start()
            to_sib(i).start()

    lane = lax.broadcasted_iota(jnp.int32, (8, T), 1)
    low_iota = lax.broadcasted_iota(jnp.int32, (T, T), 0)
    sub = lax.broadcasted_iota(jnp.int32, (8, T), 0)
    nothing = jnp.zeros((8, T), F32)

    def trees(row_lo, row_hi):
        def step(g, r):
            start = r * C + g * GROUP
            for q in range(GROUP // 8):
                rows = pl.ds(pl.multiple_of(start + q * 8, 8), 8)
                ids = species[rows, :]
                live = lane < cnt_b[rows, :]
                high = jnp.where(live, lax.shift_right_arithmetic(ids, 7) - 4 * me, -1)
                low = ids & 127
                value = growth[rows, :].astype(BF).astype(F32)

                def left_side(p):
                    chosen = jnp.broadcast_to(high[p : p + 1, :], (8, T)) == (sub & 3)
                    held_value = jnp.where(sub < 4, jnp.broadcast_to(value[p : p + 1, :], (8, T)), 1.0)
                    return jnp.where(chosen, held_value, 0.0)

                def right_side(p):
                    same = jnp.broadcast_to(low[p : p + 1, :], (T, T)) == low_iota
                    return jnp.where(same, 1.0, 0.0).astype(BF)

                for p in range(0, 8, 2):
                    a = jnp.concatenate(
                        [
                            jnp.concatenate([left_side(p), nothing], 1),
                            jnp.concatenate([nothing, left_side(p + 1)], 1),
                        ],
                        0,
                    ).astype(BF)
                    b = jnp.concatenate([right_side(p), right_side(p + 1)], 1)
                    both = lax.dot_general(a, b, (((1,), (1,)), ((), ())), preferred_element_type=F32)
                    for j in range(2):
                        sums[pl.ds(g * GROUP + q * 8 + p + j, 8, stride=C), :] = both[j * 8 : (j + 1) * 8, :]
            return r

        def whole(r, carry):
            lax.fori_loop(0, C // GROUP, step, r)
            rows = pl.ds(pl.multiple_of(r * C, C), C)
            for h in range(4):
                cs = slice(h * T, (h + 1) * T)
                total = sums[h * C : (h + 1) * C, :]
                tally = sums[(h + 4) * C : (h + 5) * C, :]
                out[rows, cs] = noise[:, cs] * (total - tally * eff[rows, cs])
            return carry

        lax.fori_loop(row_lo, row_hi, whole, 0)

    def prior(ks, start, size, steps):
        def body(i, carry):
            rows = pl.ds(pl.multiple_of(start + i * size, 256), size)
            total = None
            for k in ks:
                q = prec[pl.ds(pl.multiple_of(block(k) * W, W), W), :]
                term = jnp.dot(spat[k, rows, :], q, preferred_element_type=F32)
                total = term if total is None else total + term
            out[rows, :] = out[rows, :] - total
            return carry

        lax.fori_loop(0, steps, body, 0)

    def store(i, start, size):
        rows = pl.ds(start, size)
        return pltpu.make_async_copy(out.at[rows], out_hbm.at[rows], out_sem.at[i])

    def gram_block(k):
        def body(i, carry):
            cs = pl.ds(pl.multiple_of(i * 256, 256), 256)
            part[k, :, cs] = jnp.dot(eff_t[...], spat[k, :, cs], preferred_element_type=F32).astype(BF)
            return carry

        lax.fori_loop(0, W // 256, body, 0)

    def gram_rows(k, starts, size, cs):
        total = None
        for r in starts:
            rows = slice(r * C, (r + size) * C)
            term = jnp.dot(eff_t[:, rows], spat[k, rows, cs], preferred_element_type=F32)
            total = term if total is None else total + term
        return total

    def gram_early(k):
        def body(i, carry):
            cs = pl.ds(pl.multiple_of(i * 256, 256), 256)
            late[k - 2, :, cs] = gram_rows(k, (1,), 1, cs) + gram_rows(k, (3,), 2, cs)
            return carry

        lax.fori_loop(0, W // 256, body, 0)

    def gram_late(k):
        def body(i, carry):
            cs = pl.ds(pl.multiple_of(i * 256, 256), 256)
            total = late[k - 2, :, cs] + gram_rows(k, (0, 2, 5), 1, cs)
            part[k, :, cs] = total.astype(BF)
            return carry

        lax.fori_loop(0, W // 256, body, 0)

    def z_peer(d):
        return dev(at(y, xh, (z + d) % 4), me)

    def gz(k, d):
        src = part.at[k, pl.ds(pl.multiple_of(((z + d) % 4) * 64, 64), 64)]
        return remote(src, rz.at[d - 1, k], gz_s.at[k, d - 1], gz_r.at[k, d - 1], z_peer(d))

    def y_peer(d):
        return dev(at((y + d) % 4, xh, z), me)

    def gy(k, d):
        src = part.at[k, pl.ds(256, 256), pl.ds(pl.multiple_of(((y + d) % 4) * T, T), T)]
        return remote(src, ry.at[d - 1, k], gy_s.at[k, d - 1], gy_r.at[k, d - 1], y_peer(d))

    def gram_send(k):
        for d in (1, 2, 3):
            gz(k, d).start()
            gy(k, d).start()

    def g2y(p, d):
        return remote(
            mid0.at[p, (y + d) % 4], ry2.at[p, d - 1], g2y_s.at[p, d - 1], g2y_r.at[p, d - 1], y_peer(d)
        )

    def g2z(p, d):
        src = mid1.at[p, pl.ds(pl.multiple_of(((z + d) % 4) * 64, 64), 64)]
        return remote(src, rz2.at[p, d - 1], g2z_s.at[p, d - 1], g2z_r.at[p, d - 1], z_peer(d))

    own_rows = pl.ds(pl.multiple_of(z * 64, 64), 64)
    own_cols = pl.ds(pl.multiple_of(y * T, T), T)

    def first_sums(p):
        for k in (2 * p, 2 * p + 1):
            cs = slice((k % 2) * T, (k % 2 + 1) * T)
            for d in (1, 2, 3):
                gz(k, d).wait_recv()
            total = part[k, own_rows, :].astype(F32)
            for d in (1, 2, 3):
                total = total + rz[d - 1, k].astype(F32)
            for q in range(4):
                mid0[p, q, :, cs] = total[:, q * T : (q + 1) * T].astype(BF)
        for d in (1, 2, 3):
            g2y(p, d).start()
        for k in (2 * p, 2 * p + 1):
            cs = slice((k % 2) * T, (k % 2 + 1) * T)
            for d in (1, 2, 3):
                gy(k, d).wait_recv()
            total = part[k, 256:512, own_cols].astype(F32)
            for d in (1, 2, 3):
                total = total + ry[d - 1, k].astype(F32)
            mid1[p, :, cs] = total.astype(BF)
        for d in (1, 2, 3):
            g2z(p, d).start()

    def to_result(h, k):
        return remote(
            held.at[h, :, pl.ds(k * T, T)],
            fin.at[xh, :, own_cols],
            last_s.at[h, k],
            last_r.at[xh, y],
            dev(at(me, h, z), block(k)),
        )

    def leaves(h):
        return jnp.logical_or(h != xh, moved)

    def results(p, h):
        for k in (2 * p, 2 * p + 1):
            if k:
                to_result(h, k).start()
            else:

                @pl.when(leaves(h))
                def _():
                    to_result(h, 0).start()

                @pl.when(jnp.logical_not(leaves(h)))
                def _():
                    fin[xh, :, own_cols] = held[h, :, 0:T]

    def arrived(h, q):
        return remote(
            held.at[0, :, pl.ds(0, T)], fin.at[h, :, pl.ds(q * T, T)], last_s.at[0, 0], last_r.at[h, q], dev(sp, sib)
        )

    def second_sums(p):
        cs = slice(p * 2 * T, (p + 1) * 2 * T)
        for d in (1, 2, 3):
            g2y(p, d).wait_recv()
        total = mid0[p, y].astype(F32)
        for d in (1, 2, 3):
            total = total + ry2[p, d - 1].astype(F32)
        held[0, :, cs] = total.astype(BF)
        results(p, 0)
        for d in (1, 2, 3):
            g2z(p, d).wait_recv()
        total = mid1[p, own_rows, :].astype(F32)
        for d in (1, 2, 3):
            total = total + rz2[p, d - 1].astype(F32)
        held[1, :, cs] = total.astype(BF)
        results(p, 1)

    for r in (1, 2, 3):
        first_row(r)
    spat_row(2)
    send(0, 1)
    first_row(4)
    spat_row(3)
    send(2)
    for i, r in enumerate((1, 4)):
        far_out[i] = eff[r * C : (r + 1) * C, :].astype(BF)
        halos[4 + i].start()
    tmp[0:R, :] = counts[...].astype(F32)
    cnt_cols = tmp[...].T
    for r in range(R):
        cnt_b[r * C : (r + 1) * C, :] = jnp.broadcast_to(cnt_cols[:, r : r + 1], (C, T)).astype(jnp.int32)
    load_species.wait()
    load_growth.wait()
    trees(0, 2)

    for i in range(4):
        halos[i].wait_recv()
    tmp[0:1, :] = kap_up[R - 1 : R, :]
    tmp[1:2, :] = kap_dn[0:1, :]
    kap_edge = tmp[...].T
    kap_b[0] = jnp.broadcast_to(kap_edge[:, 0:1], (C, T)) + 4.0
    kap_b[R + 1] = jnp.broadcast_to(kap_edge[:, 1:2], (C, T)) + 4.0

    @pl.when(sp == 0)
    def _():
        near[0] = jnp.zeros((C, W), F32)

    @pl.when(sp == 31)
    def _():
        near[1] = jnp.zeros((C, W), F32)

    first_row(0)
    first_row(5)
    spat_row(1)
    spat_row(4)
    send(3, 4)
    trees(2, 3)
    pass_on(0)
    pass_on(1)
    trees(3, 4)

    halos[4].wait_recv()
    halos[5].wait_recv()
    first_row(-1)
    first_row(6)

    @pl.when(sp == 0)
    def _():
        first[0] = jnp.zeros((C, W), F32)

    @pl.when(sp == 31)
    def _():
        first[R + 1] = jnp.zeros((C, W), F32)

    spat_row(0)
    spat_row(5)
    send(5, 6)

    for r in range(R):
        eff_t[:, r * C : (r + 1) * C] = eff[r * C : (r + 1) * C, :].T.astype(BF)
    gram_block(0)
    gram_send(0)
    for i in range(NC):
        to_sib(i).wait_recv()
    gram_block(1)
    gram_send(1)
    trees(4, 6)
    load_prec.wait()
    prior((0, 1), 0, 512, 3)

    for i in (2, 3, 4):
        to_far(i).wait_recv()
        on(i).start()
    first_sums(0)
    gram_early(2)
    for i in (2, 3, 4):
        on(i).wait_recv()
    gram_early(3)
    prior((2, 3), C, C, 1)
    prior((2, 3), 4 * C, C, 1)
    store(0, C, C).start()
    store(1, 4 * C, C).start()
    second_sums(0)

    for i in (5, 6, 0, 1):
        to_far(i).wait_recv()
        on(i).start()
    gram_late(2)
    gram_send(2)
    for i in (5, 6, 0, 1):
        on(i).wait_recv()
    gram_late(3)
    gram_send(3)
    prior((2, 3), 2 * C, 2 * C, 1)
    prior((2, 3), 0, C, 1)
    prior((2, 3), 5 * C, C, 1)
    store(2, 2 * C, 2 * C).start()
    store(3, 0, C).start()
    store(4, 5 * C, C).start()

    first_sums(1)
    second_sums(1)
    for h in range(2):
        for q in range(4):

            @pl.when(jnp.logical_or(jnp.logical_or(h != xh, q != y), moved))
            def _():
                arrived(h, q).wait_recv()

    gram[...] = (fin[0].astype(F32) + fin[1].astype(F32)) * (-0.5 / (NP * 32))

    for copy in halos:
        copy.wait_send()
    for i in range(NC):
        to_sib(i).wait_send()
        to_far(i).wait_send()
        on(i).wait_send()
    for j in range(2):

        @pl.when(is_inner)
        def _():
            from_relay(0, j).wait_send()

    for d in (1, 2, 3):
        for k in range(4):
            gz(k, d).wait_send()
            gy(k, d).wait_send()
        for p in range(2):
            g2y(p, d).wait_send()
            g2z(p, d).wait_send()
    for h in range(2):
        for k in (1, 2, 3):
            to_result(h, k).wait_send()

        @pl.when(leaves(h))
        def _():
            to_result(h, 0).wait_send()

    for i, (start, size) in enumerate(((C, C), (4 * C, C), (2 * C, 2 * C), (0, C), (5 * C, C))):
        store(i, start, size).wait()


def finish(grad_in, gram_in, grad_out, gram_out, grad, gram, sem_in, sem_out):
    grad_rows = [pl.ds(r * C, C) for r in range(R)]
    loads = [pltpu.make_async_copy(grad_in.at[rows], grad.at[rows], sem_in.at[r]) for r, rows in enumerate(grad_rows)]
    loads.append(pltpu.make_async_copy(gram_in, gram, sem_in.at[R]))
    stores = [pltpu.make_async_copy(grad.at[rows], grad_out.at[rows], sem_out.at[r]) for r, rows in enumerate(grad_rows)]
    stores.append(pltpu.make_async_copy(gram, gram_out, sem_out.at[R]))
    for load in loads:
        load.start()
    for load, store in zip(loads, stores):
        load.wait()
        store.start()
    for store in stores:
        store.wait()


def shards(effects, kappa_sq, growth, tree_species, tree_counts, noise_precision, species_precision):
    vmem = pl.BlockSpec(memory_space=pltpu.VMEM)
    hbm = pl.BlockSpec(memory_space=pl.ANY)
    dma = pltpu.SemaphoreType.DMA
    grad, gram = pl.pallas_call(
        kernel,
        out_shape=(jax.ShapeDtypeStruct((NP, W), F32), jax.ShapeDtypeStruct((64, W), F32)),
        in_specs=[hbm, vmem, hbm, hbm, vmem, vmem, hbm],
        out_specs=(hbm, vmem),
        scratch_shapes=[
            pltpu.VMEM((NP, W), F32),
            pltpu.VMEM((NP, T), F32),
            pltpu.VMEM((NP, T), jnp.int32),
            pltpu.VMEM((4 * W, W), BF),
            pltpu.VMEM((NP, W), F32),
            pltpu.VMEM((2, C, W), F32),
            pltpu.VMEM((2, C, W), BF),
            pltpu.VMEM((2, C, W), BF),
            pltpu.VMEM((3 * C // 2, W), BF),
            pltpu.VMEM((R, C), F32),
            pltpu.VMEM((R, C), F32),
            pltpu.VMEM((8, C), F32),
            pltpu.VMEM((R + 2, C, T), F32),
            pltpu.VMEM((NP, T), jnp.int32),
            pltpu.VMEM((R + 2, C, W), F32),
            pltpu.VMEM((4, NP, W), BF),
            pltpu.VMEM((W, NP), BF),
            pltpu.VMEM((8 * C, T), F32),
            pltpu.VMEM((4, W, W), BF),
            pltpu.VMEM((2, W, W), F32),
            pltpu.VMEM((3, 4, 64, W), BF),
            pltpu.VMEM((3, 4, 256, T), BF),
            pltpu.VMEM((2, 4, 64, 2 * T), BF),
            pltpu.VMEM((2, 256, 2 * T), BF),
            pltpu.VMEM((2, 3, 64, 2 * T), BF),
            pltpu.VMEM((2, 3, 64, 2 * T), BF),
            pltpu.VMEM((2, 64, W), BF),
            pltpu.VMEM((2, 64, W), BF),
            dma((6,)), dma((6,)),
            dma((2,)), dma((2,)),
            dma((3, NC)), dma((3, NC)),
            dma((4, 3)), dma((4, 3)),
            dma((4, 3)), dma((4, 3)),
            dma((2, 3)), dma((2, 3)),
            dma((2, 3)), dma((2, 3)),
            dma((2, 4)), dma((2, 4)),
            dma((R + 3,)),
            dma((5,)),
        ],
        compiler_params=pltpu.CompilerParams(
            collective_id=0, has_side_effects=True, vmem_limit_bytes=56 << 20
        ),
        cost_estimate=pl.CostEstimate(flops=7_000_000_000, bytes_accessed=12_000_000, transcendentals=0),
        name="posterior_gradient",
    )(
        effects.reshape(NP, W),
        kappa_sq,
        growth.reshape(NP, T),
        tree_species.reshape(NP, T),
        tree_counts,
        noise_precision.reshape(1, W),
        species_precision,
    )
    grad, gram = pl.pallas_call(
        finish,
        out_shape=(jax.ShapeDtypeStruct((NP, W), F32), jax.ShapeDtypeStruct((64, W), F32)),
        in_specs=[hbm, hbm],
        out_specs=(hbm, hbm),
        scratch_shapes=[pltpu.VMEM((NP, W), F32), pltpu.VMEM((64, W), F32), dma((R + 1,)), dma((R + 1,))],
        compiler_params=pltpu.CompilerParams(vmem_limit_bytes=56 << 20),
        name="finish",
    )(grad, gram)
    return grad.reshape(R, C, W), gram


def solution(mesh):
    return jax.shard_map(
        shards,
        mesh=mesh,
        in_specs=(
            P("space", None, "species"),
            P("space", None),
            P("space", None, None),
            P("space", None, None),
            P("space", None),
            P("species"),
            P(None, "species"),
        ),
        out_specs=(P("space", None, "species"), P("space", "species")),
        check_vma=False,
    )
```

```python
import jax
import jax.numpy as jnp
from jax import lax
from jax.experimental import pallas as pl
from jax.experimental.pallas import tpu as pltpu
from jax.sharding import PartitionSpec as P

MESH = pl.DeviceIdType.MESH
BF = jnp.bfloat16
F32 = jnp.float32
R, C, W, T = 6, 256, 512, 128
NP = R * C
GROUP = 32
CHUNKS = ((2 * C, C), (3 * C, C // 4), (3 * C + C // 4, 3 * C // 4), (C, C), (4 * C, C), (0, C), (5 * C, C))
NC = len(CHUNKS)


def kernel(
    eff_in, kap, growth_in, species_in, counts, noise, prec_in,
    out_hbm, gram,
    eff, growth, species, prec, out,
    near, far_out, far_in, relayed, kap_up, kap_dn, tmp, kap_b, cnt_b, first, spat, eff_t, sums,
    part, late, rz, ry, mid0, mid1, rz2, ry2, held, fin,
    halo_s, halo_r, relay_s, relay_r, ex_s, ex_r, gz_s, gz_r, gy_s, gy_r, g2y_s, g2y_r, g2z_s, g2z_r, last_s, last_r, in_sem, out_sem,
):
    sp, me = lax.axis_index("space"), lax.axis_index("species")
    z, xh, y = sp % 4, (sp // 4) % 2, sp // 8
    up, dn = (sp + 31) % 32, (sp + 1) % 32
    sib = (me // 2) * 2 + (me + 1) % 2
    far = (me + 2) % 4

    def at(yy, hh, zz):
        return (yy * 2 + hh) * 4 + zz

    def dev(space, spec):
        return {"space": space, "species": spec}

    def block(k):
        return ((me // 2 + k // 2) % 2) * 2 + (me % 2 + k % 2) % 2

    moved = y != me

    def remote(src, dst, ssem, rsem, to):
        return pltpu.make_async_remote_copy(
            src_ref=src, dst_ref=dst, send_sem=ssem, recv_sem=rsem, device_id=to, device_id_type=MESH
        )

    loads = [pltpu.make_async_copy(eff_in.at[pl.ds(r * C, C)], eff.at[pl.ds(r * C, C)], in_sem.at[r]) for r in range(R)]
    for r in (1, 4, 2, 3, 0, 5):
        loads[r].start()
    load_species = pltpu.make_async_copy(species_in, species, in_sem.at[R])
    load_growth = pltpu.make_async_copy(growth_in, growth, in_sem.at[R + 1])
    load_prec = pltpu.make_async_copy(prec_in, prec, in_sem.at[R + 2])
    load_species.start()
    load_growth.start()
    load_prec.start()

    barrier = pltpu.get_barrier_semaphore()
    peers = [dev(up, me), dev(dn, me), dev(sp, sib), dev(sp, far)]
    peers += [dev(at(y, xh, (z + d) % 4), me) for d in (1, 2, 3)]
    peers += [dev(at((y + d) % 4, xh, z), me) for d in (1, 2, 3)]
    peers += [dev(at((y + d) % 4, h, z), y) for d in (1, 2, 3) for h in (0, 1)]
    peers += [dev(at(y, 1 - xh, z), y)]
    for peer in peers:
        pl.semaphore_signal(barrier, inc=1, device_id=peer, device_id_type=MESH)

    @pl.when(moved)
    def _():
        pl.semaphore_signal(barrier, inc=1, device_id=dev(sp, y), device_id_type=MESH)

    outer = (z == 0, z == 3)
    inner = (z == 1, z == 2)
    for i in range(2):

        @pl.when(outer[i])
        def _():
            pl.semaphore_signal(barrier, inc=1, device_id=dev((dn, up)[i], far), device_id_type=MESH)

    is_inner = jnp.logical_or(z == 1, z == 2)

    tmp[...] = jnp.zeros_like(tmp)
    tmp[0:R, :] = kap[...]
    kap_cols = tmp[...].T
    for r in range(R):
        kap_b[r + 1] = jnp.broadcast_to(kap_cols[:, r : r + 1], (C, T)) + 4.0

    pl.semaphore_wait(barrier, len(peers) + moved.astype(jnp.int32) + is_inner.astype(jnp.int32))

    def far_row(i):
        return remote(
            far_out.at[i], far_in.at[i], halo_s.at[4 + i], halo_r.at[4 + i], dev(up if i == 0 else dn, me)
        )

    halos = [
        remote(eff_in.at[pl.ds(0, C)], near.at[1], halo_s.at[0], halo_r.at[0], dev(up, me)),
        remote(eff_in.at[pl.ds(5 * C, C)], near.at[0], halo_s.at[1], halo_r.at[1], dev(dn, me)),
        remote(kap, kap_dn, halo_s.at[2], halo_r.at[2], dev(up, me)),
        remote(kap, kap_up, halo_s.at[3], halo_r.at[3], dev(dn, me)),
        far_row(0),
        far_row(1),
    ]
    for copy in halos[:4]:
        copy.start()
    for r in (1, 4, 2, 3, 0, 5):
        loads[r].wait()

    def erow(r):
        if 0 <= r < R:
            return eff.at[pl.ds(r * C, C)]
        return {-2: far_in.at[1], -1: near.at[0], 6: near.at[1], 7: far_in.at[0]}[r]

    edge = lax.broadcasted_iota(jnp.int32, (C, T), 0)

    def stencil(centre, above, below, kappa):
        left = jnp.where(edge == 0, 0.0, pltpu.roll(centre, 1, 0))
        right = jnp.where(edge == C - 1, 0.0, pltpu.roll(centre, C - 1, 0))
        return kappa * centre - (below + above + right + left)

    def first_row(r):
        def body(c, carry):
            cs = pl.ds(pl.multiple_of(c * T, T), T)
            first[r + 1, :, cs] = stencil(
                erow(r)[:, cs], erow(r - 1)[:, cs].astype(F32), erow(r + 1)[:, cs].astype(F32), kap_b[r + 1]
            )
            return carry

        lax.fori_loop(0, W // T, body, 0)

    def spat_row(r):
        def body(c, carry):
            cs = pl.ds(pl.multiple_of(c * T, T), T)
            s = stencil(first[r + 1, :, cs], first[r, :, cs], first[r + 2, :, cs], kap_b[r + 1])
            spat[0, r * C : (r + 1) * C, cs] = s.astype(BF)
            return carry

        lax.fori_loop(0, W // T, body, 0)

    def piece(k, i):
        return spat.at[k, pl.ds(*CHUNKS[i])]

    def to_sib(i):
        return remote(piece(0, i), piece(1, i), ex_s.at[0, i], ex_r.at[0, i], dev(sp, sib))

    def to_far(i):
        return remote(piece(0, i), piece(2, i), ex_s.at[1, i], ex_r.at[1, i], dev(sp, far))

    def on(i):
        return remote(piece(2, i), piece(3, i), ex_s.at[2, i], ex_r.at[2, i], dev(sp, sib))

    def relay(j):
        return relayed.at[pl.ds(CHUNKS[j][0] - 2 * C, CHUNKS[j][1])]

    def to_relay(i, j):
        return remote(piece(0, j), relay(j), ex_s.at[1, j], relay_r.at[j], dev((dn, up)[i], me))

    def from_relay(i, j):
        return remote(relay(j), piece(2, j), relay_s.at[j], ex_r.at[1, j], dev((up, dn)[i], far))

    def pass_on(j):
        for i in range(2):

            @pl.when(inner[i])
            def _():
                to_relay(i, j).wait_recv()
                from_relay(i, j).start()

    def send(*chunks):
        for i in chunks:
            if i < 2:
                for t in range(2):

                    @pl.when(outer[t])
                    def _():
                        to_relay(t, i).start()

                @pl.when(is_inner)
                def _():
                    to_far(i).start()

            else:
                to_far(i).start()
            to_sib(i).start()

    lane = lax.broadcasted_iota(jnp.int32, (8, T), 1)
    low_iota = lax.broadcasted_iota(jnp.int32, (T, T), 0)
    sub = lax.broadcasted_iota(jnp.int32, (8, T), 0)
    nothing = jnp.zeros((8, T), F32)

    def trees(row_lo, row_hi):
        def step(g, r):
            start = r * C + g * GROUP
            for q in range(GROUP // 8):
                rows = pl.ds(pl.multiple_of(start + q * 8, 8), 8)
                ids = species[rows, :]
                live = lane < cnt_b[rows, :]
                high = jnp.where(live, lax.shift_right_arithmetic(ids, 7) - 4 * me, -1)
                low = ids & 127
                value = growth[rows, :].astype(BF).astype(F32)

                def left_side(p):
                    chosen = jnp.broadcast_to(high[p : p + 1, :], (8, T)) == (sub & 3)
                    held_value = jnp.where(sub < 4, jnp.broadcast_to(value[p : p + 1, :], (8, T)), 1.0)
                    return jnp.where(chosen, held_value, 0.0)

                def right_side(p):
                    same = jnp.broadcast_to(low[p : p + 1, :], (T, T)) == low_iota
                    return jnp.where(same, 1.0, 0.0).astype(BF)

                for p in range(0, 8, 2):
                    a = jnp.concatenate(
                        [
                            jnp.concatenate([left_side(p), nothing], 1),
                            jnp.concatenate([nothing, left_side(p + 1)], 1),
                        ],
                        0,
                    ).astype(BF)
                    b = jnp.concatenate([right_side(p), right_side(p + 1)], 1)
                    both = lax.dot_general(a, b, (((1,), (1,)), ((), ())), preferred_element_type=F32)
                    for j in range(2):
                        sums[pl.ds(g * GROUP + q * 8 + p + j, 8, stride=C), :] = both[j * 8 : (j + 1) * 8, :]
            return r

        def whole(r, carry):
            lax.fori_loop(0, C // GROUP, step, r)
            rows = pl.ds(pl.multiple_of(r * C, C), C)
            for h in range(4):
                cs = slice(h * T, (h + 1) * T)
                total = sums[h * C : (h + 1) * C, :]
                tally = sums[(h + 4) * C : (h + 5) * C, :]
                out[rows, cs] = noise[:, cs] * (total - tally * eff[rows, cs])
            return carry

        lax.fori_loop(row_lo, row_hi, whole, 0)

    def prior(ks, start, size, steps):
        def body(i, carry):
            rows = pl.ds(pl.multiple_of(start + i * size, 256), size)
            total = None
            for k in ks:
                q = prec[pl.ds(pl.multiple_of(block(k) * W, W), W), :]
                term = jnp.dot(spat[k, rows, :], q, preferred_element_type=F32)
                total = term if total is None else total + term
            out[rows, :] = out[rows, :] - total
            return carry

        lax.fori_loop(0, steps, body, 0)

    def store(i, start, size):
        rows = pl.ds(start, size)
        return pltpu.make_async_copy(out.at[rows], out_hbm.at[rows], out_sem.at[i])

    def gram_block(k):
        def body(i, carry):
            cs = pl.ds(pl.multiple_of(i * 256, 256), 256)
            part[k, :, cs] = jnp.dot(eff_t[...], spat[k, :, cs], preferred_element_type=F32).astype(BF)
            return carry

        lax.fori_loop(0, W // 256, body, 0)

    def gram_rows(k, starts, size, cs):
        total = None
        for r in starts:
            rows = slice(r * C, (r + size) * C)
            term = jnp.dot(eff_t[:, rows], spat[k, rows, cs], preferred_element_type=F32)
            total = term if total is None else total + term
        return total

    def gram_early(k):
        def body(i, carry):
            cs = pl.ds(pl.multiple_of(i * 256, 256), 256)
            late[k - 2, :, cs] = gram_rows(k, (1, 4), 1, cs)
            return carry

        lax.fori_loop(0, W // 256, body, 0)

    def gram_late(k):
        def body(i, carry):
            cs = pl.ds(pl.multiple_of(i * 256, 256), 256)
            total = late[k - 2, :, cs] + gram_rows(k, (2,), 2, cs) + gram_rows(k, (0, 5), 1, cs)
            part[k, :, cs] = total.astype(BF)
            return carry

        lax.fori_loop(0, W // 256, body, 0)

    def z_peer(d):
        return dev(at(y, xh, (z + d) % 4), me)

    def gz(k, d):
        src = part.at[k, pl.ds(pl.multiple_of(((z + d) % 4) * 64, 64), 64)]
        return remote(src, rz.at[d - 1, k], gz_s.at[k, d - 1], gz_r.at[k, d - 1], z_peer(d))

    def y_peer(d):
        return dev(at((y + d) % 4, xh, z), me)

    def gy(k, d):
        src = part.at[k, pl.ds(256, 256), pl.ds(pl.multiple_of(((y + d) % 4) * T, T), T)]
        return remote(src, ry.at[d - 1, k], gy_s.at[k, d - 1], gy_r.at[k, d - 1], y_peer(d))

    def gram_send(k):
        for d in (1, 2, 3):
            gz(k, d).start()
            gy(k, d).start()

    def g2y(p, d):
        return remote(
            mid0.at[p, (y + d) % 4], ry2.at[p, d - 1], g2y_s.at[p, d - 1], g2y_r.at[p, d - 1], y_peer(d)
        )

    def g2z(p, d):
        src = mid1.at[p, pl.ds(pl.multiple_of(((z + d) % 4) * 64, 64), 64)]
        return remote(src, rz2.at[p, d - 1], g2z_s.at[p, d - 1], g2z_r.at[p, d - 1], z_peer(d))

    own_rows = pl.ds(pl.multiple_of(z * 64, 64), 64)
    own_cols = pl.ds(pl.multiple_of(y * T, T), T)

    def first_sums(p):
        for k in (2 * p, 2 * p + 1):
            cs = slice((k % 2) * T, (k % 2 + 1) * T)
            for d in (1, 2, 3):
                gz(k, d).wait_recv()
            total = part[k, own_rows, :].astype(F32)
            for d in (1, 2, 3):
                total = total + rz[d - 1, k].astype(F32)
            for q in range(4):
                mid0[p, q, :, cs] = total[:, q * T : (q + 1) * T].astype(BF)
        for d in (1, 2, 3):
            g2y(p, d).start()
        for k in (2 * p, 2 * p + 1):
            cs = slice((k % 2) * T, (k % 2 + 1) * T)
            for d in (1, 2, 3):
                gy(k, d).wait_recv()
            total = part[k, 256:512, own_cols].astype(F32)
            for d in (1, 2, 3):
                total = total + ry[d - 1, k].astype(F32)
            mid1[p, :, cs] = total.astype(BF)
        for d in (1, 2, 3):
            g2z(p, d).start()

    def to_result(h, k):
        return remote(
            held.at[h, :, pl.ds(k * T, T)],
            fin.at[xh, :, own_cols],
            last_s.at[h, k],
            last_r.at[xh, y],
            dev(at(me, h, z), block(k)),
        )

    def leaves(h):
        return jnp.logical_or(h != xh, moved)

    def results(p, h):
        for k in (2 * p, 2 * p + 1):
            if k:
                to_result(h, k).start()
            else:

                @pl.when(leaves(h))
                def _():
                    to_result(h, 0).start()

                @pl.when(jnp.logical_not(leaves(h)))
                def _():
                    fin[xh, :, own_cols] = held[h, :, 0:T]

    def arrived(h, q):
        return remote(
            held.at[0, :, pl.ds(0, T)], fin.at[h, :, pl.ds(q * T, T)], last_s.at[0, 0], last_r.at[h, q], dev(sp, sib)
        )

    def second_sums(p):
        cs = slice(p * 2 * T, (p + 1) * 2 * T)
        for d in (1, 2, 3):
            g2y(p, d).wait_recv()
        total = mid0[p, y].astype(F32)
        for d in (1, 2, 3):
            total = total + ry2[p, d - 1].astype(F32)
        held[0, :, cs] = total.astype(BF)
        results(p, 0)
        for d in (1, 2, 3):
            g2z(p, d).wait_recv()
        total = mid1[p, own_rows, :].astype(F32)
        for d in (1, 2, 3):
            total = total + rz2[p, d - 1].astype(F32)
        held[1, :, cs] = total.astype(BF)
        results(p, 1)

    for r in (1, 2, 3):
        first_row(r)
    spat_row(2)
    send(0)
    first_row(4)
    spat_row(3)
    send(2, 1)
    for i, r in enumerate((1, 4)):
        far_out[i] = eff[r * C : (r + 1) * C, :].astype(BF)
        halos[4 + i].start()
    tmp[0:R, :] = counts[...].astype(F32)
    cnt_cols = tmp[...].T
    for r in range(R):
        cnt_b[r * C : (r + 1) * C, :] = jnp.broadcast_to(cnt_cols[:, r : r + 1], (C, T)).astype(jnp.int32)
    load_species.wait()
    load_growth.wait()
    trees(0, 2)

    for i in range(4):
        halos[i].wait_recv()
    tmp[0:1, :] = kap_up[R - 1 : R, :]
    tmp[1:2, :] = kap_dn[0:1, :]
    kap_edge = tmp[...].T
    kap_b[0] = jnp.broadcast_to(kap_edge[:, 0:1], (C, T)) + 4.0
    kap_b[R + 1] = jnp.broadcast_to(kap_edge[:, 1:2], (C, T)) + 4.0

    @pl.when(sp == 0)
    def _():
        near[0] = jnp.zeros((C, W), F32)

    @pl.when(sp == 31)
    def _():
        near[1] = jnp.zeros((C, W), F32)

    first_row(0)
    first_row(5)
    spat_row(1)
    spat_row(4)
    send(3, 4)
    trees(2, 3)
    pass_on(0)
    pass_on(1)
    trees(3, 4)

    halos[4].wait_recv()
    halos[5].wait_recv()
    first_row(-1)
    first_row(6)

    @pl.when(sp == 0)
    def _():
        first[0] = jnp.zeros((C, W), F32)

    @pl.when(sp == 31)
    def _():
        first[R + 1] = jnp.zeros((C, W), F32)

    spat_row(0)
    spat_row(5)
    send(5, 6)

    for r in range(R):
        eff_t[:, r * C : (r + 1) * C] = eff[r * C : (r + 1) * C, :].T.astype(BF)
    gram_block(0)
    gram_send(0)
    for i in range(NC):
        to_sib(i).wait_recv()
    gram_block(1)
    gram_send(1)
    trees(4, 6)
    load_prec.wait()
    prior((0, 1), 0, 512, 3)

    for i in (2, 3, 4):
        to_far(i).wait_recv()
        on(i).start()
    first_sums(0)
    gram_early(2)
    for i in (2, 3, 4):
        on(i).wait_recv()
    gram_early(3)
    prior((2, 3), C, C, 1)
    prior((2, 3), 4 * C, C, 1)
    store(0, C, C).start()
    store(1, 4 * C, C).start()
    second_sums(0)

    for i in (5, 6, 0, 1):
        to_far(i).wait_recv()
        on(i).start()
    gram_late(2)
    gram_send(2)
    for i in (5, 6, 0, 1):
        on(i).wait_recv()
    gram_late(3)
    gram_send(3)
    prior((2, 3), 2 * C, 2 * C, 1)
    prior((2, 3), 0, C, 1)
    prior((2, 3), 5 * C, C, 1)
    store(2, 2 * C, 2 * C).start()
    store(3, 0, C).start()
    store(4, 5 * C, C).start()

    first_sums(1)
    second_sums(1)
    for h in range(2):
        for q in range(4):

            @pl.when(jnp.logical_or(jnp.logical_or(h != xh, q != y), moved))
            def _():
                arrived(h, q).wait_recv()

    gram[...] = (fin[0].astype(F32) + fin[1].astype(F32)) * (-0.5 / (NP * 32))

    for copy in halos:
        copy.wait_send()
    for i in range(NC):
        to_sib(i).wait_send()
        to_far(i).wait_send()
        on(i).wait_send()
    for j in range(2):

        @pl.when(is_inner)
        def _():
            from_relay(0, j).wait_send()

    for d in (1, 2, 3):
        for k in range(4):
            gz(k, d).wait_send()
            gy(k, d).wait_send()
        for p in range(2):
            g2y(p, d).wait_send()
            g2z(p, d).wait_send()
    for h in range(2):
        for k in (1, 2, 3):
            to_result(h, k).wait_send()

        @pl.when(leaves(h))
        def _():
            to_result(h, 0).wait_send()

    for i, (start, size) in enumerate(((C, C), (4 * C, C), (2 * C, 2 * C), (0, C), (5 * C, C))):
        store(i, start, size).wait()


def finish(grad_in, gram_in, grad_out, gram_out, grad, gram, sem_in, sem_out):
    grad_rows = [pl.ds(r * C, C) for r in range(R)]
    loads = [pltpu.make_async_copy(grad_in.at[rows], grad.at[rows], sem_in.at[r]) for r, rows in enumerate(grad_rows)]
    loads.append(pltpu.make_async_copy(gram_in, gram, sem_in.at[R]))
    stores = [pltpu.make_async_copy(grad.at[rows], grad_out.at[rows], sem_out.at[r]) for r, rows in enumerate(grad_rows)]
    stores.append(pltpu.make_async_copy(gram, gram_out, sem_out.at[R]))
    for load in loads:
        load.start()
    for load, store in zip(loads, stores):
        load.wait()
        store.start()
    for store in stores:
        store.wait()


def shards(effects, kappa_sq, growth, tree_species, tree_counts, noise_precision, species_precision):
    vmem = pl.BlockSpec(memory_space=pltpu.VMEM)
    hbm = pl.BlockSpec(memory_space=pl.ANY)
    dma = pltpu.SemaphoreType.DMA
    grad, gram = pl.pallas_call(
        kernel,
        out_shape=(jax.ShapeDtypeStruct((NP, W), F32), jax.ShapeDtypeStruct((64, W), F32)),
        in_specs=[hbm, vmem, hbm, hbm, vmem, vmem, hbm],
        out_specs=(hbm, vmem),
        scratch_shapes=[
            pltpu.VMEM((NP, W), F32),
            pltpu.VMEM((NP, T), F32),
            pltpu.VMEM((NP, T), jnp.int32),
            pltpu.VMEM((4 * W, W), BF),
            pltpu.VMEM((NP, W), F32),
            pltpu.VMEM((2, C, W), F32),
            pltpu.VMEM((2, C, W), BF),
            pltpu.VMEM((2, C, W), BF),
            pltpu.VMEM((3 * C // 2, W), BF),
            pltpu.VMEM((R, C), F32),
            pltpu.VMEM((R, C), F32),
            pltpu.VMEM((8, C), F32),
            pltpu.VMEM((R + 2, C, T), F32),
            pltpu.VMEM((NP, T), jnp.int32),
            pltpu.VMEM((R + 2, C, W), F32),
            pltpu.VMEM((4, NP, W), BF),
            pltpu.VMEM((W, NP), BF),
            pltpu.VMEM((8 * C, T), F32),
            pltpu.VMEM((4, W, W), BF),
            pltpu.VMEM((2, W, W), F32),
            pltpu.VMEM((3, 4, 64, W), BF),
            pltpu.VMEM((3, 4, 256, T), BF),
            pltpu.VMEM((2, 4, 64, 2 * T), BF),
            pltpu.VMEM((2, 256, 2 * T), BF),
            pltpu.VMEM((2, 3, 64, 2 * T), BF),
            pltpu.VMEM((2, 3, 64, 2 * T), BF),
            pltpu.VMEM((2, 64, W), BF),
            pltpu.VMEM((2, 64, W), BF),
            dma((6,)), dma((6,)),
            dma((2,)), dma((2,)),
            dma((3, NC)), dma((3, NC)),
            dma((4, 3)), dma((4, 3)),
            dma((4, 3)), dma((4, 3)),
            dma((2, 3)), dma((2, 3)),
            dma((2, 3)), dma((2, 3)),
            dma((2, 4)), dma((2, 4)),
            dma((R + 3,)),
            dma((5,)),
        ],
        compiler_params=pltpu.CompilerParams(
            collective_id=0, has_side_effects=True, vmem_limit_bytes=56 << 20
        ),
        cost_estimate=pl.CostEstimate(flops=7_000_000_000, bytes_accessed=12_000_000, transcendentals=0),
        name="posterior_gradient",
    )(
        effects.reshape(NP, W),
        kappa_sq,
        growth.reshape(NP, T),
        tree_species.reshape(NP, T),
        tree_counts,
        noise_precision.reshape(1, W),
        species_precision,
    )
    grad, gram = pl.pallas_call(
        finish,
        out_shape=(jax.ShapeDtypeStruct((NP, W), F32), jax.ShapeDtypeStruct((64, W), F32)),
        in_specs=[hbm, hbm],
        out_specs=(hbm, hbm),
        scratch_shapes=[pltpu.VMEM((NP, W), F32), pltpu.VMEM((64, W), F32), dma((R + 1,)), dma((R + 1,))],
        compiler_params=pltpu.CompilerParams(vmem_limit_bytes=56 << 20),
        name="finish",
    )(grad, gram)
    return grad.reshape(R, C, W), gram


def solution(mesh):
    return jax.shard_map(
        shards,
        mesh=mesh,
        in_specs=(
            P("space", None, "species"),
            P("space", None),
            P("space", None, None),
            P("space", None, None),
            P("space", None),
            P("species"),
            P(None, "species"),
        ),
        out_specs=(P("space", None, "species"), P("space", "species")),
        check_vma=False,
    )
```
